512 devices in a mesh: era: 8 (over x, core), dp: 64 (over y, z).
Axes of the slice: x: 4, y: 8, z: 8, core: 2. Of those that a mesh axis runs over, the one named last changes fastest.
Arguments:
- counts: int32 [7680, 128, 128], P(('era', 'dp')), may hold values from 0 to 4, as said below
- block_term: int32 [7680], P(('era', 'dp')), may hold values from 0 to 63, as said below
- doc_year: int32 [65536], P(('era', 'dp')), may hold values from 0 to 15, as said below
- doc_topics: bfloat16 [65536, 256], P(('era', 'dp')), may hold values from 0.019897461 to 1
- log_params: float32 [16, 256, 8192], P('era', None, 'dp'), may hold values from -12 to 12
- drift: float32 [256], replicated, may hold values from 0.02 to 0.5
- obs_noise: float32 [256], replicated, may hold values from 0.2 to 2
Outputs:
- new_topics: bfloat16 [65536, 256], P(('era', 'dp'))
- smoothed: float32 [16, 256, 8192], P('era', None, 'dp')
The draws below stay inside these ranges and needn't reach their ends.
Inputs may be any that keep to these rules, and one draw needn't show every extreme that they name: `counts`: every document has a count of 1 or more in the first term column of its device's first block that covers it. `block_term`: the 15 blocks of one document block name distinct term blocks. `doc_year`: all documents of one device share one year; the devices of era index e hold years e * 2 to e * 2 + 1, each of these years on equally many devices.
All inputs are finite; a program needn't handle non-finite values.
Results may differ from the reference program's by a relative error of at most 0.0049.
Values may be sent and summed in bfloat16 or wider, within the bound.
A program may use at most 64 MiB of HBM per device.

```python
import math
import jax
import jax.numpy as jnp
from jax import lax

K = 256
V_DEV = 128
P_DEV = 2
BPR = 15
DOC_BLOCKS = 1
YEARS = 16
V = 8192
DOCS = 65536
N_ERA = 8
N_DP = 64


def draw_counts(key, part):
    key = jax.random.fold_in(key, 11)
    total = DOC_BLOCKS * BPR * N_ERA * N_DP
    values = jax.random.randint(key, (total, 128, 128), 0, 5)
    leading = jnp.arange(total) % BPR == 0
    column_zero = jnp.arange(128) == 0
    floor_one = jnp.where(leading[:, None, None] & column_zero[None, None, :], 1, 0)
    return jnp.maximum(values, floor_one).astype(jnp.int32)


def draw_block_term(key, part):
    key = jax.random.fold_in(key, 23)
    groups_all = DOC_BLOCKS * N_ERA * N_DP
    tblocks = V_DEV * N_DP // 128
    subkeys = jax.random.split(key, groups_all)

    def shuffle(subkey):
        return jax.random.permutation(subkey, tblocks)
    orders = jax.vmap(shuffle)(subkeys)
    return orders[:, :BPR].reshape(groups_all * BPR).astype(jnp.int32)


def draw_doc_year(key, part):
    key = jax.random.fold_in(key, 37)
    subkeys = jax.random.split(key, N_ERA)

    def ranking(subkey):
        return jax.random.permutation(subkey, N_DP)
    ranks = jax.vmap(ranking)(subkeys)
    offsets = ranks // (N_DP // P_DEV)
    years = jnp.arange(N_ERA)[:, None] * P_DEV + offsets
    return jnp.repeat(years.reshape(N_ERA * N_DP), DOC_BLOCKS * 128).astype(jnp.int32)


def block_scale(own_key, extent, cuts, low, top_value):
    gain, own = 1.0, jax.random.fold_in(own_key, 6)
    for position, blocks in cuts:
        draws = jnp.exp(jax.random.uniform(jax.random.fold_in(own, position), (blocks,), jnp.float32, low / len(cuts), top_value / len(cuts)))
        gain = gain * jnp.repeat(draws, extent[position] // blocks).reshape([-1 if axis == position else 1 for axis in range(len(extent))])
    return gain


def bell_draw(rng, extent, width, reach, cuts=(), kind=jnp.bfloat16):
    level = block_scale(rng, extent, cuts, -0.22, 0.18) if cuts else 1.0
    drawn = jax.random.normal(rng, extent, jnp.float32) * width * level
    return jnp.minimum(jnp.maximum(drawn, -reach), reach).astype(kind)


def setup_inputs(seed: int = 0) -> dict:
    arg_keys = jax.random.split(jax.random.key(seed), 8)
    return {
        "counts": draw_counts(jax.random.fold_in(arg_keys[7], 71), 0),
        "block_term": draw_block_term(jax.random.fold_in(arg_keys[7], 71), 0),
        "doc_year": draw_doc_year(jax.random.fold_in(arg_keys[7], 71), 0),
        "doc_topics": jnp.clip(jnp.exp(math.log(1.0) - 3.9171631 * jax.random.uniform(arg_keys[3], (DOCS, K), jnp.float32) ** block_scale(arg_keys[3], (DOCS, K), ((0, 512),), -0.2, 0.2)), 0.019897461, 1.0).astype(jnp.bfloat16),
        "log_params": bell_draw(arg_keys[4], (YEARS, K, V), 3.0, 12.0, ((0, 8), (2, 64)), jnp.float32),
        "drift": jnp.clip(jnp.exp(jax.random.uniform(arg_keys[5], (K,), jnp.float32, math.log(0.02), math.log(0.5))), 0.02, 0.5),
        "obs_noise": jnp.clip(jnp.exp(jax.random.uniform(arg_keys[6], (K,), jnp.float32, math.log(0.2), math.log(2.0))), 0.2, 2.0),
    }


def reference(counts, block_term, doc_year, doc_topics, log_params, drift, obs_noise):
    terms = V_DEV * N_DP
    tblocks = terms // 128
    device_count = N_ERA * N_DP
    nblk = DOC_BLOCKS * BPR
    ndoc = DOC_BLOCKS * 128
    exponent = jnp.exp(log_params)
    normalizer = jnp.sum(exponent, axis=2, keepdims=True)
    word_probs = lax.optimization_barrier((exponent / normalizer).astype(jnp.bfloat16))
    proportion = doc_topics.astype(jnp.float32)
    proportion = proportion / jnp.sum(proportion, axis=1, keepdims=True)
    proportion_low = lax.optimization_barrier(proportion.astype(jnp.bfloat16))

    def device_step(statistics, index):
        blocks = lax.dynamic_slice_in_dim(counts, index * nblk, nblk, 0).astype(jnp.float32)
        columns = lax.dynamic_slice_in_dim(block_term, index * nblk, nblk, 0).astype(jnp.int32)
        doc_rows = lax.dynamic_slice_in_dim(proportion_low, index * ndoc, ndoc, 0).astype(jnp.float32)
        weights = lax.dynamic_slice_in_dim(proportion, index * ndoc, ndoc, 0)
        year_index = lax.dynamic_index_in_dim(doc_year, index * ndoc, 0, keepdims=False).astype(jnp.int32)
        word_table = lax.dynamic_index_in_dim(word_probs, year_index, 0, keepdims=False)
        tiles = word_table.reshape(K, tblocks, 128)[:, columns, :].astype(jnp.float32)
        tiles = tiles.reshape(K, DOC_BLOCKS, BPR, 128)
        left_rows = doc_rows.reshape(DOC_BLOCKS, 128, K)
        scores = jnp.einsum('gdk,kgbw->gbdw', left_rows, tiles)
        quotient = blocks.reshape(DOC_BLOCKS, BPR, 128, 128) / scores
        ratios = lax.optimization_barrier(quotient.astype(jnp.bfloat16)).astype(jnp.float32)
        partial_value = jnp.einsum('gdk,gbdw->kgbw', left_rows, ratios) * tiles
        pull_back = jnp.einsum('gbdw,kgbw->gdk', ratios, tiles).reshape(ndoc, K)
        doc_length = jnp.sum(blocks.reshape(DOC_BLOCKS, BPR, 128, 128), axis=(1, 3)).reshape(ndoc)
        fresh = (K * weights * pull_back / doc_length[:, None]).astype(jnp.bfloat16)
        update = jnp.transpose(partial_value.reshape(K, nblk, 128), (1, 0, 2))
        statistics = statistics.at[year_index, :, columns, :].add(update)
        return statistics, fresh

    start = jnp.zeros((YEARS, K, tblocks, 128), jnp.float32)
    statistics, fresh_rows = lax.scan(device_step, start, jnp.arange(device_count, dtype=jnp.int32))
    new_topics = fresh_rows.reshape(device_count * ndoc, K)
    statistics = statistics.reshape(YEARS, K, terms)
    year_totals = jnp.sum(statistics, axis=2, keepdims=True)
    observed = jnp.log(statistics + 1.0) + jnp.log(float(terms)) - jnp.log(year_totals + terms)
    noise_var = obs_noise[None, :, None] / (1.0 + jnp.log(1.0 + statistics))
    spread = drift[:, None]
    variance_now = jnp.full((K, terms), 1.0, jnp.float32)
    mean_now = jnp.zeros((K, terms), jnp.float32)
    means = []
    variances = []
    for period in range(YEARS):
        predicted = variance_now + spread
        gain_now = predicted / (predicted + noise_var[period])
        mean_now = mean_now + gain_now * (observed[period] - mean_now)
        variance_now = predicted * noise_var[period] / (predicted + noise_var[period])
        means.append(mean_now)
        variances.append(variance_now)
    smooth_now = means[-1]
    results = [smooth_now]
    for period in range(YEARS - 2, -1, -1):
        weight_now = variances[period] / (variances[period] + spread)
        smooth_now = means[period] + weight_now * (smooth_now - means[period])
        results.insert(0, smooth_now)
    return new_topics, jnp.stack(results)
```

```python
import functools

import jax
import jax.numpy as jnp
from jax import lax
from jax.experimental import pallas as pl
from jax.experimental.pallas import tpu as pltpu
from jax.sharding import PartitionSpec as P

MESH = pl.DeviceIdType.MESH
NZ = 8
PRIOR_VARIANCE = 1.0
BLOCK = 128


def dot(a, b, contract):
    return lax.dot_general(a, b, (contract, ((), ())), preferred_element_type=jnp.float32)


def row_sums(value):
    turned = jnp.transpose(value)
    total = turned[0:8]
    for start in range(8, turned.shape[0], 8):
        total = total + turned[start : start + 8]
    return total


class Exchange:
    def __init__(self, buffer, send_sems, recv_sems, me, count, target):
        self.buffer, self.send_sems, self.recv_sems = buffer, send_sems, recv_sems
        self.me, self.count, self.target = me, count, target

    def copy(self, offset):
        peer = lax.rem(self.me + offset, self.count)
        return pltpu.make_async_remote_copy(
            src_ref=self.buffer.at[self.me],
            dst_ref=self.buffer.at[self.me],
            send_sem=self.send_sems.at[offset - 1],
            recv_sem=self.recv_sems.at[offset - 1],
            device_id=self.target(peer),
            device_id_type=MESH,
        )

    def start(self):
        for offset in range(1, self.count):
            self.copy(offset).start()

    def wait_recv(self):
        for offset in range(1, self.count):
            self.copy(offset).wait_recv()

    def wait_send(self):
        for offset in range(1, self.count):
            self.copy(offset).wait_send()

    def total(self):
        total = self.buffer[0]
        for slot in range(1, self.count):
            total = total + self.buffer[slot]
        return total


def kernel(
    sizes,
    bterm,
    dyear,
    counts,
    topics,
    logp,
    drift,
    onoise,
    new_ref,
    out_ref,
    pb,
    cnt,
    mbuf,
    msmem,
    expo,
    wbuf,
    nzb,
    nyb,
    scale,
    ptall,
    rall,
    pbs,
    pbr,
    sts,
    str_,
    tzb,
    tyb,
    teb,
    cmat,
    cturn,
    es,
    er,
    sm,
    ring_send,
    ring_recv,
    m_send,
    m_recv,
    w_send,
    w_recv,
    nz_send,
    nz_recv,
    ny_send,
    ny_recv,
    pb_send,
    pb_recv,
    st_send,
    st_recv,
    tz_send,
    tz_recv,
    ty_send,
    ty_recv,
    te_send,
    te_recv,
    es_send,
    es_recv,
    out_send,
    out_recv,
    local_sem,
):
    ne, ny, nz, years, k, nblk, pieces = sizes
    rows = years * k
    era = lax.axis_index("era")
    dp = lax.axis_index("dp")
    y = dp // nz
    z = lax.rem(dp, nz)

    def at_z(peer):
        return {"dp": y * nz + peer}

    def at_y(peer):
        return {"dp": peer * nz + z}

    def at_era(peer):
        return {"era": peer}

    barrier = pltpu.get_barrier_semaphore()
    for offset in range(1, nz):
        pl.semaphore_signal(barrier, inc=1, device_id=at_z(lax.rem(z + offset, nz)), device_id_type=MESH)
    for offset in range(1, ny):
        pl.semaphore_signal(barrier, inc=1, device_id=at_y(lax.rem(y + offset, ny)), device_id_type=MESH)
    for offset in range(1, ne):
        pl.semaphore_signal(barrier, inc=1, device_id=at_era(lax.rem(era + offset, ne)), device_id_type=MESH)
    pl.semaphore_wait(barrier, nz + ny + ne - 3)

    exponent = jnp.exp(logp[...].reshape(rows, BLOCK))
    expo[...] = exponent
    nzb[z] = row_sums(exponent)
    norm_z = Exchange(nzb, nz_send, nz_recv, z, nz, at_z)
    norm_z.start()

    lane = lax.broadcasted_iota(jnp.int32, (8, BLOCK), 1)
    place = jnp.full((8, BLOCK), nblk, jnp.int32)
    for index in range(nblk):
        place = jnp.where(lane == bterm[index], index, place)
    place = jnp.where(lane == ny * nz, lax.rem(dyear[0], years), place)
    mbuf[z] = place
    meta = Exchange(mbuf, m_send, m_recv, z, nz, at_z)
    meta.start()

    proportion = topics[...].astype(jnp.float32)
    proportion = proportion / jnp.sum(proportion, axis=1, keepdims=True)
    pb[z] = proportion.astype(jnp.bfloat16)
    per_piece = nblk // pieces
    hops = nz // 2
    items = pieces + 1
    first_half = list(range(items // 2))
    second_half = list(range(items // 2, items))

    def ring_items(way, hop):
        if hop < hops - 1:
            return list(range(items))
        return first_half if way == 0 else second_half

    def ring_copy(way, hop, item):
        if way == 0:
            slot, peer = lax.rem(z - hop + nz, nz), lax.rem(z + 1, nz)
        else:
            slot, peer = lax.rem(z + hop, nz), lax.rem(z + nz - 1, nz)
        if item == 0:
            ref = pb.at[slot]
        else:
            ref = cnt.at[slot, pl.ds((item - 1) * per_piece, per_piece)]
        return pltpu.make_async_remote_copy(
            src_ref=ref,
            dst_ref=ref,
            send_sem=ring_send.at[way, hop, item],
            recv_sem=ring_recv.at[way, hop, item],
            device_id=at_z(peer),
            device_id_type=MESH,
        )

    length = jnp.zeros((BLOCK, BLOCK), jnp.int32)
    for item in range(items):
        if item > 0:
            for index in range((item - 1) * per_piece, item * per_piece):
                value = counts[index]
                length = length + value
                cnt[z, index] = value.astype(jnp.float32).astype(jnp.bfloat16)
        for way in range(2):
            if item in ring_items(way, 0):
                ring_copy(way, 0, item).start()
    for slot in range(nz):
        cnt[slot, nblk] = jnp.zeros((BLOCK, BLOCK), jnp.bfloat16)
    doc_length = jnp.sum(length.astype(jnp.float32), axis=1, keepdims=True)
    scale[...] = float(k) * proportion / doc_length

    norm_z.wait_recv()
    nyb[y] = norm_z.total()
    norm_y = Exchange(nyb, ny_send, ny_recv, y, ny, at_y)
    norm_y.start()
    norm_y.wait_recv()
    normalizer = jnp.sum(norm_y.total(), axis=0, keepdims=True)
    normalizer = jnp.transpose(jnp.broadcast_to(normalizer, (BLOCK, rows)))
    own_columns = pl.ds(pl.multiple_of(y * BLOCK, BLOCK), BLOCK)
    wbuf[:, :, own_columns] = (expo[...] / normalizer).astype(jnp.bfloat16).reshape(years, k, BLOCK)

    def word_copy(offset):
        ref = wbuf.at[:, :, own_columns]
        return pltpu.make_async_remote_copy(
            src_ref=ref,
            dst_ref=ref,
            send_sem=w_send.at[offset - 1],
            recv_sem=w_recv.at[offset - 1],
            device_id=at_y(lax.rem(y + offset, ny)),
            device_id_type=MESH,
        )

    for offset in range(1, ny):
        word_copy(offset).start()
    meta.wait_recv()
    to_smem = pltpu.make_async_copy(mbuf, msmem, local_sem)
    to_smem.start()

    for hop in range(hops):
        for item in range(items):
            for way in range(2):
                if item in ring_items(way, hop):
                    ring_copy(way, hop, item).wait_recv()
                    if hop + 1 < hops and item in ring_items(way, hop + 1):
                        ring_copy(way, hop + 1, item).start()
    to_smem.wait()
    for offset in range(1, ny):
        word_copy(offset).wait_recv()

    def pull_copy(offset):
        return pltpu.make_async_remote_copy(
            src_ref=pbs.at[lax.rem(z + offset, nz)],
            dst_ref=pbr.at[z],
            send_sem=pb_send.at[offset - 1],
            recv_sem=pb_recv.at[offset - 1],
            device_id=at_z(lax.rem(z + offset, nz)),
            device_id_type=MESH,
        )

    def document_block(source):
        year = msmem[source, 0, ny * nz]
        low = pb[source]
        table = wbuf[year]
        scores = dot(low, table, ((1,), (0,)))
        parts = []
        for column in range(ny):
            block = cnt[source, msmem[source, 0, column * nz + z]].astype(jnp.float32)
            parts.append((block / scores[:, column * BLOCK : (column + 1) * BLOCK]).astype(jnp.bfloat16))
        ratios = jnp.concatenate(parts, axis=1)
        here = pl.ds(pl.multiple_of(source * BLOCK, BLOCK), BLOCK)
        rall[here, :] = ratios
        turned = jnp.transpose(low.astype(jnp.float32))
        for period in range(years):
            flag = (year == period).astype(jnp.float32)
            ptall[period * k : (period + 1) * k, here] = (turned * flag).astype(jnp.bfloat16)
        pull = dot(ratios, table, ((1,), (1,)))
        return pull.astype(jnp.bfloat16)

    def document_step(offset, carry):
        source = lax.rem(z + offset, nz)
        pbs[source] = document_block(source)
        pull_copy(offset).start()
        return carry

    lax.fori_loop(1, nz, document_step, 0)
    pbr[z] = document_block(z)

    def stat_copy(offset):
        return pltpu.make_async_remote_copy(
            src_ref=sts.at[lax.rem(y + offset, ny)],
            dst_ref=str_.at[y],
            send_sem=st_send.at[offset - 1],
            recv_sem=st_recv.at[offset - 1],
            device_id=at_y(lax.rem(y + offset, ny)),
            device_id_type=MESH,
        )

    def stat_block(owner):
        columns = pl.ds(pl.multiple_of(owner * BLOCK, BLOCK), BLOCK)
        part = dot(ptall[...], rall[:, columns], ((1,), (0,)))
        return part * wbuf[:, :, columns].reshape(rows, BLOCK).astype(jnp.float32)

    part = stat_block(y)
    str_[y] = part.astype(jnp.bfloat16)
    expo[...] = part

    def stat_step(offset, carry):
        owner = lax.rem(y + offset, ny)
        part = stat_block(owner)
        sts[owner] = part.astype(jnp.bfloat16)
        expo[...] += part
        stat_copy(offset).start()
        return carry

    lax.fori_loop(1, ny, stat_step, 0)

    tzb[z] = row_sums(expo[...])
    total_z = Exchange(tzb, tz_send, tz_recv, z, nz, at_z)
    total_z.start()
    total_z.wait_recv()
    tyb[y] = total_z.total()
    total_y = Exchange(tyb, ty_send, ty_recv, y, ny, at_y)
    total_y.start()

    for offset in range(1, nz):
        pull_copy(offset).wait_recv()
    pull = pbr[0].astype(jnp.float32)
    for slot in range(1, nz):
        pull = pull + pbr[slot].astype(jnp.float32)
    new_ref[...] = (scale[...] * pull).astype(jnp.bfloat16)

    total_y.wait_recv()
    terms = float(ny * nz * BLOCK)
    year_totals = jnp.sum(total_y.total(), axis=0, keepdims=True)
    level = jnp.log(terms) - jnp.log(year_totals + terms)
    teb[era] = jnp.broadcast_to(level, (8, rows))
    total_era = Exchange(teb, te_send, te_recv, era, ne, at_era)
    total_era.start()
    cmat[...] = jnp.zeros_like(cmat)
    all_years = ne * years
    cmat[all_years : all_years + 1, :] = drift[...]
    cmat[all_years + 1 : all_years + 2, :] = onoise[...]
    total_era.wait_recv()
    for index in range(ne):
        for period in range(years):
            cmat[index * years + period : index * years + period + 1, :] = teb[index, 0:1, period * k : (period + 1) * k]
    cturn[...] = jnp.transpose(cmat[...])

    for offset in range(1, ny):
        stat_copy(offset).wait_recv()
    own = str_[0].astype(jnp.float32)
    for slot in range(1, ny):
        own = own + str_[slot].astype(jnp.float32)
    slice_rows = k // ne
    es[...] = jnp.log(own + 1.0).reshape(years, k, BLOCK)

    def slice_of(peer):
        return pl.ds(pl.multiple_of(peer * slice_rows, slice_rows), slice_rows)

    def era_copy(offset):
        peer = lax.rem(era + offset, ne)
        return pltpu.make_async_remote_copy(
            src_ref=es.at[:, slice_of(peer)],
            dst_ref=er.at[era],
            send_sem=es_send.at[offset - 1],
            recv_sem=es_recv.at[offset - 1],
            device_id=at_era(peer),
            device_id_type=MESH,
        )

    for offset in range(1, ne):
        era_copy(offset).start()
    er[era] = es[:, slice_of(era), :]
    columns = cturn[slice_of(era), :]

    def column(index):
        return jnp.broadcast_to(columns[:, index : index + 1], (slice_rows, BLOCK))

    spread = column(all_years)
    noise_scale = column(all_years + 1)
    for offset in range(1, ne):
        era_copy(offset).wait_recv()

    variance = jnp.full((slice_rows, BLOCK), PRIOR_VARIANCE, jnp.float32)
    mean = jnp.zeros((slice_rows, BLOCK), jnp.float32)
    means, weights = [], []
    for period in range(all_years):
        level = er[period // years, period % years]
        observed = level + column(period)
        noise = noise_scale / (1.0 + level)
        predicted = variance + spread
        gain = predicted / (predicted + noise)
        mean = mean + gain * (observed - mean)
        variance = gain * noise
        means.append(mean)
        weights.append(variance / (variance + spread))
    smooth = means[-1]
    sm[ne - 1, years - 1] = smooth
    for period in range(all_years - 2, -1, -1):
        smooth = means[period] + weights[period] * (smooth - means[period])
        sm[period // years, period % years] = smooth

    def out_copy(offset):
        peer = lax.rem(era + offset, ne)
        return pltpu.make_async_remote_copy(
            src_ref=sm.at[peer],
            dst_ref=out_ref.at[:, slice_of(era)],
            send_sem=out_send.at[offset - 1],
            recv_sem=out_recv.at[offset - 1],
            device_id=at_era(peer),
            device_id_type=MESH,
        )

    for offset in range(1, ne):
        out_copy(offset).start()
    keep = pltpu.make_async_copy(sm.at[era], out_ref.at[:, slice_of(era)], local_sem)
    keep.start()
    norm_z.wait_send()
    meta.wait_send()
    norm_y.wait_send()
    total_z.wait_send()
    total_y.wait_send()
    total_era.wait_send()
    for hop in range(hops):
        for item in range(items):
            for way in range(2):
                if item in ring_items(way, hop):
                    ring_copy(way, hop, item).wait_send()
    for offset in range(1, ny):
        word_copy(offset).wait_send()
        stat_copy(offset).wait_send()
    for offset in range(1, nz):
        pull_copy(offset).wait_send()
    for offset in range(1, ne):
        era_copy(offset).wait_send()
    keep.wait()
    for offset in range(1, ne):
        out_copy(offset).wait_send()
        out_copy(offset).wait_recv()


def body(counts, block_term, doc_year, doc_topics, log_params, drift, obs_noise):
    ne = lax.axis_size("era")
    dp_count = lax.axis_size("dp")
    nz = NZ
    ny = dp_count // nz
    years, k, _ = log_params.shape
    rows = years * k
    nblk = counts.shape[0]
    pieces = next(count for count in (5, 3, 2, 1) if nblk % count == 0)
    sizes = (ne, ny, nz, years, k, nblk, pieces)
    bf16, f32, i32 = jnp.bfloat16, jnp.float32, jnp.int32
    dma = pltpu.SemaphoreType.DMA
    vmem = pl.BlockSpec(memory_space=pltpu.VMEM)
    smem = pl.BlockSpec(memory_space=pltpu.SMEM)
    hops = nz // 2
    new_topics, smoothed = pl.pallas_call(
        functools.partial(kernel, sizes),
        out_shape=(
            jax.ShapeDtypeStruct(doc_topics.shape, bf16),
            jax.ShapeDtypeStruct(log_params.shape, f32),
        ),
        in_specs=[smem, smem, vmem, vmem, vmem, vmem, vmem],
        out_specs=(vmem, pl.BlockSpec(memory_space=pl.ANY)),
        scratch_shapes=[
            pltpu.VMEM((nz, BLOCK, k), bf16),
            pltpu.VMEM((nz, nblk + 1, BLOCK, BLOCK), bf16),
            pltpu.VMEM((nz, 8, BLOCK), i32),
            pltpu.SMEM((nz, 8, BLOCK), i32),
            pltpu.VMEM((rows, BLOCK), f32),
            pltpu.VMEM((years, k, ny * BLOCK), bf16),
            pltpu.VMEM((nz, 8, rows), f32),
            pltpu.VMEM((ny, 8, rows), f32),
            pltpu.VMEM((BLOCK, k), f32),
            pltpu.VMEM((rows, nz * BLOCK), bf16),
            pltpu.VMEM((nz * BLOCK, ny * BLOCK), bf16),
            pltpu.VMEM((nz, BLOCK, k), bf16),
            pltpu.VMEM((nz, BLOCK, k), bf16),
            pltpu.VMEM((ny, rows, BLOCK), bf16),
            pltpu.VMEM((ny, rows, BLOCK), bf16),
            pltpu.VMEM((nz, 8, rows), f32),
            pltpu.VMEM((ny, 8, rows), f32),
            pltpu.VMEM((ne, 8, rows), f32),
            pltpu.VMEM((BLOCK, k), f32),
            pltpu.VMEM((k, BLOCK), f32),
            pltpu.VMEM((years, k, BLOCK), f32),
            pltpu.VMEM((ne, years, k // ne, BLOCK), f32),
            pltpu.VMEM((ne, years, k // ne, BLOCK), f32),
            dma((2, hops, pieces + 1)),
            dma((2, hops, pieces + 1)),
            dma((nz,)),
            dma((nz,)),
            dma((ny,)),
            dma((ny,)),
            dma((nz,)),
            dma((nz,)),
            dma((ny,)),
            dma((ny,)),
            dma((nz,)),
            dma((nz,)),
            dma((ny,)),
            dma((ny,)),
            dma((nz,)),
            dma((nz,)),
            dma((ny,)),
            dma((ny,)),
            dma((ne,)),
            dma((ne,)),
            dma((ne,)),
            dma((ne,)),
            dma((ne,)),
            dma((ne,)),
            dma,
        ],
        compiler_params=pltpu.CompilerParams(
            collective_id=0, has_side_effects=True, vmem_limit_bytes=48 * 1024 * 1024
        ),
    )(
        block_term,
        doc_year,
        counts,
        doc_topics,
        log_params,
        drift.reshape(1, -1),
        obs_noise.reshape(1, -1),
    )
    return (new_topics, smoothed)


def solution(mesh):
    return jax.shard_map(
        body,
        mesh=mesh,
        in_specs=(
            P(("era", "dp"), None, None),
            P(("era", "dp")),
            P(("era", "dp")),
            P(("era", "dp"), None),
            P("era", None, "dp"),
            P(),
            P(),
        ),
        out_specs=(P(("era", "dp"), None), P("era", None, "dp")),
        check_vma=False,
    )
```

```python
import functools

import jax
import jax.numpy as jnp
from jax import lax
from jax.experimental import pallas as pl
from jax.experimental.pallas import tpu as pltpu
from jax.sharding import PartitionSpec as P

MESH = pl.DeviceIdType.MESH
NZ = 8
PRIOR_VARIANCE = 1.0
BLOCK = 128


def dot(a, b, contract):
    return lax.dot_general(a, b, (contract, ((), ())), preferred_element_type=jnp.float32)


def row_sums(value):
    return jnp.sum(jnp.transpose(value), axis=0, keepdims=True)


class Copies:
    def __init__(self, copies):
        self.copies = copies

    def start(self):
        for copy in self.copies:
            copy.start()

    def wait_recv(self):
        for copy in self.copies:
            copy.wait_recv()

    def wait_send(self):
        for copy in self.copies:
            copy.wait_send()


def remote(src, dst, send_sem, recv_sem, device):
    return pltpu.make_async_remote_copy(
        src_ref=src, dst_ref=dst, send_sem=send_sem, recv_sem=recv_sem, device_id=device, device_id_type=MESH
    )


def kernel(sizes, *refs):
    ne, ny, nz, years, k, nblk, pieces = sizes
    refs = list(refs)

    def take(count=None):
        if count is None:
            return refs.pop(0)
        return [refs.pop(0) for _ in range(count)]

    bterm_in, dyear_in, counts_in, topics_in, logp_in, drift_in, onoise_in = take(7)
    new_ref, out_ref = take(2)
    bterm, dyear, counts, topics, logp, drift, onoise = take(7)
    low = take(nz)
    cnt = take(nz)
    mbuf, msmem, expo, wbuf, nzb, nyb, scale, ptall, rall = take(9)
    pbs, pbr, sts, str_, tyb, tzb, teb, cmat, cturn, es, er, sm = take(12)
    in_sems, ring_send, ring_recv, local_sem = take(4)
    pairs = [take(2) for _ in range(len(refs) // 2)]
    m_sems, w_sems, nz_sems, ny_sems, pb_sems, st_sems, ty_sems, tz_sems, te_sems, es_sems, out_sems = pairs

    rows = years * k
    all_years = ne * years
    slice_rows = k // ne
    era = lax.axis_index("era")
    dp = lax.axis_index("dp")
    y = dp // nz
    z = lax.rem(dp, nz)

    def at_z(offset):
        return {"dp": y * nz + lax.rem(z + offset, nz)}

    def at_y(offset):
        return {"dp": lax.rem(y + offset, ny) * nz + z}

    def at_era(offset):
        return {"era": lax.rem(era + offset, ne)}

    def spread_out(buffer, me, count, target, sems):
        send, recv = sems
        return Copies(
            [
                remote(buffer.at[me], buffer.at[me], send.at[offset - 1], recv.at[offset - 1], target(offset))
                for offset in range(1, count)
            ]
        )

    def total_of(buffer, count):
        total = buffer[0].astype(jnp.float32)
        for slot in range(1, count):
            total = total + buffer[slot].astype(jnp.float32)
        return total

    barrier = pltpu.get_barrier_semaphore()
    for target, count in ((at_z, nz), (at_y, ny), (at_era, ne)):
        for offset in range(1, count):
            pl.semaphore_signal(barrier, inc=1, device_id=target(offset), device_id_type=MESH)
    inputs = (
        (logp_in, logp),
        (topics_in, topics),
        (counts_in, counts),
        (bterm_in, bterm),
        (dyear_in, dyear),
        (drift_in, drift),
        (onoise_in, onoise),
    )
    loads = [pltpu.make_async_copy(src, dst, in_sems.at[index]) for index, (src, dst) in enumerate(inputs)]
    for load in loads:
        load.start()

    loads[0].wait()
    exponent = jnp.exp(logp[...].reshape(rows, BLOCK))
    expo[...] = exponent
    nzb[z] = row_sums(exponent)
    loads[1].wait()
    proportion = topics[...].astype(jnp.float32)
    proportion = proportion / jnp.sum(proportion, axis=1, keepdims=True)
    low[0][...] = proportion.astype(jnp.bfloat16)
    for load in loads[3:]:
        load.wait()
    lane = lax.broadcasted_iota(jnp.int32, (8, BLOCK), 1)
    place = jnp.full((8, BLOCK), nblk, jnp.int32)
    for index in range(nblk):
        place = jnp.where(lane == bterm[index], index, place)
    place = jnp.where(lane == ny * nz, lax.rem(dyear[0], years), place)
    mbuf[z] = place
    loads[2].wait()

    norm_z = spread_out(nzb, z, nz, at_z, nz_sems)
    norm_y = spread_out(nyb, y, ny, at_y, ny_sems)
    meta = spread_out(mbuf, z, nz, at_z, m_sems)

    per_piece = nblk // pieces
    hops = nz // 2
    items = pieces + 1

    def ring_items(way, hop):
        if hop < hops - 1:
            return list(range(items))
        return list(range(items // 2)) if way == 0 else list(range(items // 2, items))

    def ring_copy(way, hop, item):
        here = hop if way else (nz - hop) % nz
        there = hop + 1 if way else nz - hop - 1
        if item == 0:
            src, dst = low[here], low[there]
        else:
            block = pl.ds((item - 1) * per_piece, per_piece)
            src, dst = cnt[here].at[block], cnt[there].at[block]
        return remote(
            src, dst, ring_send.at[way, hop, item], ring_recv.at[way, hop, item], at_z(nz - 1 if way else 1)
        )

    def ring_pass(hop, which):
        for item in which:
            for way in range(2):
                if item in ring_items(way, hop):
                    ring_copy(way, hop, item).wait_recv()
                    if hop + 1 < hops and item in ring_items(way, hop + 1):
                        ring_copy(way, hop + 1, item).start()

    length = jnp.zeros((BLOCK, BLOCK), jnp.int32)
    for index in range(nblk):
        value = counts[index]
        length = length + value
        cnt[0][index] = value.astype(jnp.float32).astype(jnp.bfloat16)
    pl.semaphore_wait(barrier, nz + ny + ne - 3)
    norm_z.start()
    meta.start()
    for item in range(items):
        for way in range(2):
            if item in ring_items(way, 0):
                ring_copy(way, 0, item).start()
    for slot in range(nz):
        cnt[slot][nblk] = jnp.zeros((BLOCK, BLOCK), jnp.bfloat16)
    doc_length = jnp.sum(length.astype(jnp.float32), axis=1, keepdims=True)
    scale[...] = float(k) * proportion / doc_length
    cmat[...] = jnp.zeros_like(cmat)
    cmat[all_years : all_years + 1, :] = drift[...]
    cmat[all_years + 1 : all_years + 2, :] = onoise[...]

    norm_z.wait_recv()
    nyb[y] = total_of(nzb, nz)
    norm_y.start()
    norm_y.wait_recv()
    normalizer = jnp.transpose(jnp.broadcast_to(total_of(nyb, ny), (BLOCK, rows)))
    own_columns = pl.ds(pl.multiple_of(y * BLOCK, BLOCK), BLOCK)
    wbuf[:, :, own_columns] = (expo[...] / normalizer).astype(jnp.bfloat16).reshape(years, k, BLOCK)
    own_words = wbuf.at[:, :, own_columns]
    words = Copies(
        [
            remote(own_words, own_words, w_sems[0].at[offset - 1], w_sems[1].at[offset - 1], at_y(offset))
            for offset in range(1, ny)
        ]
    )
    words.start()
    meta.wait_recv()
    to_smem = pltpu.make_async_copy(mbuf, msmem, local_sem)
    to_smem.start()
    to_smem.wait()

    totals = [jnp.zeros((1, k), jnp.float32) for _ in range(years)]

    def document_block(slot):
        source = lax.rem(z + slot, nz)
        year = msmem[source, 0, ny * nz]
        left = low[slot][...]
        table = wbuf[year]
        scores = dot(left, table, ((1,), (0,)))
        here = slice(slot * BLOCK, (slot + 1) * BLOCK)
        for column in range(ny):
            block = cnt[slot][msmem[source, 0, column * nz + z]].astype(jnp.float32)
            terms = slice(column * BLOCK, (column + 1) * BLOCK)
            rall[here, terms] = (block / scores[:, terms]).astype(jnp.bfloat16)
        pull = dot(rall[here, :], table, ((1,), (1,)))
        left = left.astype(jnp.float32)
        share = jnp.sum(left * pull, axis=0, keepdims=True)
        turned = jnp.transpose(left)
        for period in range(years):
            flag = (year == period).astype(jnp.float32)
            ptall[period * k : (period + 1) * k, here] = (turned * flag).astype(jnp.bfloat16)
            totals[period] = totals[period] + share * flag
        if slot == 0:
            pbr[z] = pull.astype(jnp.bfloat16)
        else:
            pbs[slot] = pull.astype(jnp.bfloat16)

    order = [0]
    for step in range(1, hops):
        order += [step, nz - step]
    order.append(hops)
    done = 0
    for hop in range(hops):
        last = hop == hops - 2 or hops == 1
        if last:
            ring_pass(hop, range(items // 2))
            words.wait_recv()
            while done < min(3, 2 * hop + 1):
                document_block(order[done])
                done += 1
            ring_pass(hop, range(items // 2, items))
        else:
            ring_pass(hop, range(items))
        if hop >= hops - 2:
            ready = nz if hop == hops - 1 else 2 * hop + 3
            while done < ready:
                document_block(order[done])
                done += 1

    tyb[y] = jnp.concatenate(totals, axis=1)
    total_y = spread_out(tyb, y, ny, at_y, ty_sems)
    total_z = spread_out(tzb, z, nz, at_z, tz_sems)
    total_era = spread_out(teb, era, ne, at_era, te_sems)
    total_y.start()

    def stat_copy(offset):
        return remote(
            sts.at[offset], str_.at[y], st_sems[0].at[offset - 1], st_sems[1].at[offset - 1], at_y(offset)
        )

    def stat_block(offset):
        columns = pl.ds(pl.multiple_of(lax.rem(y + offset, ny) * BLOCK, BLOCK), BLOCK)
        part = dot(ptall[...], rall[:, columns], ((1,), (0,)))
        part = part * wbuf[:, :, columns].reshape(rows, BLOCK).astype(jnp.float32)
        return part.astype(jnp.bfloat16)

    def stat_step(offset, carry):
        sts[offset] = stat_block(offset)
        stat_copy(offset).start()
        return carry

    lax.fori_loop(1, ny, stat_step, 0)
    str_[y] = stat_block(0)
    stats = Copies([stat_copy(offset) for offset in range(1, ny)])
    total_y.wait_recv()
    tzb[z] = total_of(tyb, ny)
    total_z.start()
    pulls = Copies(
        [
            remote(pbs.at[offset], pbr.at[z], pb_sems[0].at[offset - 1], pb_sems[1].at[offset - 1], at_z(offset))
            for offset in range(1, nz)
        ]
    )
    pulls.start()
    total_z.wait_recv()
    terms = float(ny * nz * BLOCK)
    teb[era] = jnp.log(terms) - jnp.log(total_of(tzb, nz) + terms)
    total_era.start()
    total_era.wait_recv()
    for index in range(ne):
        for period in range(years):
            cmat[index * years + period : index * years + period + 1, :] = teb[index, :, period * k : (period + 1) * k]
    cturn[...] = jnp.transpose(cmat[...])

    stats.wait_recv()
    es[...] = total_of(str_, ny).astype(jnp.bfloat16).reshape(years, k, BLOCK)

    def slice_of(offset):
        return pl.ds(pl.multiple_of(lax.rem(era + offset, ne) * slice_rows, slice_rows), slice_rows)

    own_slice = slice_of(0)
    levels = Copies(
        [
            remote(
                es.at[:, slice_of(offset)],
                er.at[era],
                es_sems[0].at[offset - 1],
                es_sems[1].at[offset - 1],
                at_era(offset),
            )
            for offset in range(1, ne)
        ]
    )
    levels.start()
    er[era] = es[:, own_slice, :]
    columns = cturn[own_slice, :]

    def column(index):
        return jnp.broadcast_to(columns[:, index : index + 1], (slice_rows, BLOCK))

    spread = column(all_years)
    noise_scale = column(all_years + 1)
    pulls.wait_recv()
    new_ref[...] = (scale[...] * total_of(pbr, nz)).astype(jnp.bfloat16)
    levels.wait_recv()

    variance = jnp.full((slice_rows, BLOCK), PRIOR_VARIANCE, jnp.float32)
    mean = jnp.zeros((slice_rows, BLOCK), jnp.float32)
    means, weights = [], []
    for period in range(all_years):
        level = jnp.log(er[period // years, period % years].astype(jnp.float32) + 1.0)
        observed = level + column(period)
        noise = noise_scale / (1.0 + level)
        predicted = variance + spread
        gain = predicted / (predicted + noise)
        mean = mean + gain * (observed - mean)
        variance = gain * noise
        means.append(mean)
        weights.append(variance / (variance + spread))
    smooth = means[-1]
    sm[ne - 1, years - 1] = smooth.astype(sm.dtype)
    for period in range(all_years - 2, -1, -1):
        smooth = means[period] + weights[period] * (smooth - means[period])
        sm[period // years, period % years] = smooth.astype(sm.dtype)

    keep = pltpu.make_async_copy(sm.at[era], out_ref.at[:, own_slice], local_sem)
    keep.start()
    results = Copies(
        [
            remote(
                sm.at[lax.rem(era + offset, ne)],
                out_ref.at[:, own_slice],
                out_sems[0].at[offset - 1],
                out_sems[1].at[offset - 1],
                at_era(offset),
            )
            for offset in range(1, ne)
        ]
    )
    results.start()
    for sent in (norm_z, meta, norm_y, words, total_y, total_z, total_era, stats, pulls, levels):
        sent.wait_send()
    for hop in range(hops):
        for item in range(items):
            for way in range(2):
                if item in ring_items(way, hop):
                    ring_copy(way, hop, item).wait_send()
    keep.wait()
    results.wait_send()
    results.wait_recv()


def body(counts, block_term, doc_year, doc_topics, log_params, drift, obs_noise):
    ne = lax.axis_size("era")
    nz = NZ
    ny = lax.axis_size("dp") // nz
    years, k, _ = log_params.shape
    rows = years * k
    nblk = counts.shape[0]
    pieces = next(count for count in (5, 3, 2, 1) if nblk % count == 0)
    sizes = (ne, ny, nz, years, k, nblk, pieces)
    bf16, f32, i32 = jnp.bfloat16, jnp.float32, jnp.int32
    hops = nz // 2
    hbm = pl.BlockSpec(memory_space=pltpu.HBM)
    operands = (
        block_term,
        doc_year,
        counts,
        doc_topics,
        log_params,
        drift.reshape(1, -1),
        obs_noise.reshape(1, -1),
    )
    landing = [
        (pltpu.SMEM if index < 2 else pltpu.VMEM)(value.shape, value.dtype) for index, value in enumerate(operands)
    ]
    slots = [pltpu.VMEM((BLOCK, k), bf16)] * nz + [pltpu.VMEM((nblk + 1, BLOCK, BLOCK), bf16)] * nz
    work = [
        pltpu.VMEM((nz, 8, BLOCK), i32),
        pltpu.SMEM((nz, 8, BLOCK), i32),
        pltpu.VMEM((rows, BLOCK), f32),
        pltpu.VMEM((years, k, ny * BLOCK), bf16),
        pltpu.VMEM((nz, 1, rows), f32),
        pltpu.VMEM((ny, 1, rows), f32),
        pltpu.VMEM((BLOCK, k), f32),
        pltpu.VMEM((rows, nz * BLOCK), bf16),
        pltpu.VMEM((nz * BLOCK, ny * BLOCK), bf16),
        pltpu.VMEM((nz, BLOCK, k), bf16),
        pltpu.VMEM((nz, BLOCK, k), bf16),
        pltpu.VMEM((ny, rows, BLOCK), bf16),
        pltpu.VMEM((ny, rows, BLOCK), bf16),
        pltpu.VMEM((ny, 1, rows), f32),
        pltpu.VMEM((nz, 1, rows), f32),
        pltpu.VMEM((ne, 1, rows), f32),
        pltpu.VMEM((BLOCK, k), f32),
        pltpu.VMEM((k, BLOCK), f32),
        pltpu.VMEM((years, k, BLOCK), bf16),
        pltpu.VMEM((ne, years, k // ne, BLOCK), bf16),
        pltpu.VMEM((ne, years, k // ne, BLOCK), bf16),
    ]
    dma = pltpu.SemaphoreType.DMA
    ring_sems = dma((2, hops, pieces + 1))
    sems = [dma((len(operands),)), ring_sems, ring_sems, dma]
    for count in (nz, ny, nz, ny, nz, ny, ny, nz, ne, ne, ne):
        sems += [dma((count - 1,))] * 2
    new_topics, smoothed = pl.pallas_call(
        functools.partial(kernel, sizes),
        out_shape=(
            jax.ShapeDtypeStruct(doc_topics.shape, bf16),
            jax.ShapeDtypeStruct(log_params.shape, bf16),
        ),
        in_specs=[hbm] * len(operands),
        out_specs=(pl.BlockSpec(memory_space=pltpu.VMEM), pl.BlockSpec(memory_space=pl.ANY)),
        scratch_shapes=landing + slots + work + sems,
        compiler_params=pltpu.CompilerParams(
            collective_id=0, has_side_effects=True, vmem_limit_bytes=48 * 1024 * 1024
        ),
    )(*operands)
    return (new_topics, smoothed.astype(f32))


def solution(mesh):
    return jax.shard_map(
        body,
        mesh=mesh,
        in_specs=(
            P(("era", "dp"), None, None),
            P(("era", "dp")),
            P(("era", "dp")),
            P(("era", "dp"), None),
            P("era", None, "dp"),
            P(),
            P(),
        ),
        out_specs=(P(("era", "dp"), None), P("era", None, "dp")),
        check_vma=False,
    )
```

```python
import functools

import jax
import jax.numpy as jnp
from jax import lax
from jax.experimental import pallas as pl
from jax.experimental.pallas import tpu as pltpu
from jax.sharding import PartitionSpec as P

MESH = pl.DeviceIdType.MESH
NZ = 8
PRIOR_VARIANCE = 1.0
BLOCK = 128
SUBS = 4


def dot(a, b, contract):
    return lax.dot_general(a, b, (contract, ((), ())), preferred_element_type=jnp.float32)


def row_sums(value):
    return jnp.sum(jnp.transpose(value), axis=0, keepdims=True)


class Copies:
    def __init__(self, copies):
        self.copies = copies

    def start(self):
        for copy in self.copies:
            copy.start()

    def wait_recv(self):
        for copy in self.copies:
            copy.wait_recv()

    def wait_send(self):
        for copy in self.copies:
            copy.wait_send()


def remote(src, dst, send_sem, recv_sem, device):
    return pltpu.make_async_remote_copy(
        src_ref=src, dst_ref=dst, send_sem=send_sem, recv_sem=recv_sem, device_id=device, device_id_type=MESH
    )


def kernel(sizes, *refs):
    ne, ny, nz, years, k, nblk, pieces = sizes
    refs = list(refs)

    def take(count=None):
        if count is None:
            return refs.pop(0)
        return [refs.pop(0) for _ in range(count)]

    bterm_in, dyear_in, counts_in, topics_in, logp_in, drift_in, onoise_in = take(7)
    new_ref, out_ref = take(2)
    bterm, dyear, counts, topics, logp, drift, onoise = take(7)
    low = take(nz)
    cnt = take(nz)
    mbuf, msmem, expo, wbuf, nzb, nyb, scale, ptall, rall = take(9)
    pbs, pbr, sts, str_, tyb, tzb, teb, cmat, cturn, es, er, sm = take(12)
    in_sems, ring_send, ring_recv, local_sem = take(4)
    pairs = [take(2) for _ in range(len(refs) // 2)]
    m_sems, w_sems, nz_sems, ny_sems, pb_sems, st_sems, ty_sems, tz_sems, te_sems, es_sems, out_sems = pairs

    rows = years * k
    all_years = ne * years
    slice_rows = k // ne
    era = lax.axis_index("era")
    dp = lax.axis_index("dp")
    y = dp // nz
    z = lax.rem(dp, nz)

    def at_z(offset):
        return {"dp": y * nz + lax.rem(z + offset, nz)}

    def at_y(offset):
        return {"dp": lax.rem(y + offset, ny) * nz + z}

    def at_era(offset):
        return {"era": lax.rem(era + offset, ne)}

    def spread_out(buffer, me, count, target, sems):
        send, recv = sems
        return Copies(
            [
                remote(buffer.at[me], buffer.at[me], send.at[offset - 1], recv.at[offset - 1], target(offset))
                for offset in range(1, count)
            ]
        )

    def total_of(buffer, count):
        total = buffer[0].astype(jnp.float32)
        for slot in range(1, count):
            total = total + buffer[slot].astype(jnp.float32)
        return total

    barrier = pltpu.get_barrier_semaphore()
    for target, count in ((at_z, nz), (at_y, ny), (at_era, ne)):
        for offset in range(1, count):
            pl.semaphore_signal(barrier, inc=1, device_id=target(offset), device_id_type=MESH)
    inputs = (
        (logp_in, logp),
        (topics_in, topics),
        (counts_in, counts),
        (bterm_in, bterm),
        (dyear_in, dyear),
        (drift_in, drift),
        (onoise_in, onoise),
    )
    loads = [pltpu.make_async_copy(src, dst, in_sems.at[index]) for index, (src, dst) in enumerate(inputs)]
    for load in loads:
        load.start()

    loads[0].wait()
    exponent = jnp.exp(logp[...].reshape(rows, BLOCK))
    expo[...] = exponent
    nzb[z] = row_sums(exponent)
    loads[1].wait()
    proportion = topics[...].astype(jnp.float32)
    proportion = proportion / jnp.sum(proportion, axis=1, keepdims=True)
    low[0][...] = proportion.astype(jnp.bfloat16)
    for load in loads[3:]:
        load.wait()
    lane = lax.broadcasted_iota(jnp.int32, (8, BLOCK), 1)
    place = jnp.full((8, BLOCK), nblk, jnp.int32)
    for index in range(nblk):
        place = jnp.where(lane == bterm[index], index, place)
    place = jnp.where(lane == ny * nz, lax.rem(dyear[0], years), place)
    mbuf[z] = place
    loads[2].wait()

    norm_z = spread_out(nzb, z, nz, at_z, nz_sems)
    norm_y = spread_out(nyb, y, ny, at_y, ny_sems)
    meta = spread_out(mbuf, z, nz, at_z, m_sems)

    per_piece = nblk // pieces
    hops = nz // 2
    items = pieces + 1

    def ring_items(way, hop):
        if hop < hops - 1:
            return list(range(items))
        return list(range(items // 2)) if way == 0 else list(range(items // 2, items))

    def ring_copy(way, hop, item):
        here = hop if way else (nz - hop) % nz
        there = hop + 1 if way else nz - hop - 1
        if item == 0:
            src, dst = low[here], low[there]
        else:
            block = pl.ds((item - 1) * per_piece, per_piece)
            src, dst = cnt[here].at[block], cnt[there].at[block]
        return remote(
            src, dst, ring_send.at[way, hop, item], ring_recv.at[way, hop, item], at_z(nz - 1 if way else 1)
        )

    def ring_pass(hop, which):
        for item in which:
            for way in range(2):
                if item in ring_items(way, hop):
                    ring_copy(way, hop, item).wait_recv()
                    if hop + 1 < hops and item in ring_items(way, hop + 1):
                        ring_copy(way, hop + 1, item).start()

    length = jnp.zeros((BLOCK, BLOCK), jnp.int32)
    for index in range(nblk):
        value = counts[index]
        length = length + value
        cnt[0][index] = value.astype(jnp.float32).astype(jnp.bfloat16)
    pl.semaphore_wait(barrier, nz + ny + ne - 3)
    norm_z.start()
    meta.start()
    for item in range(items):
        for way in range(2):
            if item in ring_items(way, 0):
                ring_copy(way, 0, item).start()
    for slot in range(nz):
        cnt[slot][nblk] = jnp.zeros((BLOCK, BLOCK), jnp.bfloat16)
    doc_length = jnp.sum(length.astype(jnp.float32), axis=1, keepdims=True)
    scale[...] = float(k) * proportion / doc_length
    cmat[...] = jnp.zeros_like(cmat)
    cmat[all_years : all_years + 1, :] = drift[...]
    cmat[all_years + 1 : all_years + 2, :] = onoise[...]

    norm_z.wait_recv()
    nyb[y] = total_of(nzb, nz)
    norm_y.start()
    norm_y.wait_recv()
    normalizer = jnp.transpose(jnp.broadcast_to(total_of(nyb, ny), (BLOCK, rows)))
    own_columns = pl.ds(pl.multiple_of(y * BLOCK, BLOCK), BLOCK)
    wbuf[:, :, own_columns] = (expo[...] / normalizer).astype(jnp.bfloat16).reshape(years, k, BLOCK)
    own_words = wbuf.at[:, :, own_columns]
    words = Copies(
        [
            remote(own_words, own_words, w_sems[0].at[offset - 1], w_sems[1].at[offset - 1], at_y(offset))
            for offset in range(1, ny)
        ]
    )
    words.start()
    meta.wait_recv()
    to_smem = pltpu.make_async_copy(mbuf, msmem, local_sem)
    to_smem.start()
    to_smem.wait()

    totals = [jnp.zeros((1, k), jnp.float32) for _ in range(years)]

    def document_block(slot):
        source = lax.rem(z + slot, nz)
        year = msmem[source, 0, ny * nz]
        left = low[slot][...]
        table = wbuf[year]
        scores = dot(left, table, ((1,), (0,)))
        here = slice(slot * BLOCK, (slot + 1) * BLOCK)
        for column in range(ny):
            block = cnt[slot][msmem[source, 0, column * nz + z]].astype(jnp.float32)
            terms = slice(column * BLOCK, (column + 1) * BLOCK)
            rall[here, terms] = (block / scores[:, terms]).astype(jnp.bfloat16)
        pull = dot(rall[here, :], table, ((1,), (1,)))
        left = left.astype(jnp.float32)
        share = jnp.sum(left * pull, axis=0, keepdims=True)
        turned = jnp.transpose(left)
        for period in range(years):
            flag = (year == period).astype(jnp.float32)
            ptall[period * k : (period + 1) * k, here] = (turned * flag).astype(jnp.bfloat16)
            totals[period] = totals[period] + share * flag
        if slot == 0:
            pbr[z] = pull.astype(jnp.bfloat16)
        else:
            pbs[slot] = pull.astype(jnp.bfloat16)

    order = [0]
    for step in range(1, hops):
        order += [step, nz - step]
    order.append(hops)
    done = 0
    for hop in range(hops):
        last = hop == hops - 2 or hops == 1
        if last:
            ring_pass(hop, range(items // 2))
            words.wait_recv()
            while done < min(3, 2 * hop + 1):
                document_block(order[done])
                done += 1
            ring_pass(hop, range(items // 2, items))
        else:
            ring_pass(hop, range(items))
        if hop >= hops - 2:
            ready = nz if hop == hops - 1 else 2 * hop + 3
            while done < ready:
                document_block(order[done])
                done += 1

    tyb[y] = jnp.concatenate(totals, axis=1)
    total_y = spread_out(tyb, y, ny, at_y, ty_sems)
    total_z = spread_out(tzb, z, nz, at_z, tz_sems)
    total_era = spread_out(teb, era, ne, at_era, te_sems)
    total_y.start()

    stat_hops = ny // 2
    sub_rows = rows // SUBS

    def stat_subs(way, hop):
        if hop > 0:
            return list(range(SUBS))
        return list(range(SUBS // 2)) if way == 0 else list(range(SUBS // 2, SUBS))

    def stat_copy(way, hop, sub):
        part = pl.ds(sub * sub_rows, sub_rows)
        return remote(
            sts.at[way, hop, part],
            str_.at[way, hop, part],
            st_sems[0].at[way, hop, sub],
            st_sems[1].at[way, hop, sub],
            at_y(ny - 1 if way else 1),
        )

    def stat_block(offset):
        columns = pl.ds(pl.multiple_of(lax.rem(y + offset, ny) * BLOCK, BLOCK), BLOCK)
        part = dot(ptall[...], rall[:, columns], ((1,), (0,)))
        return part * wbuf[:, :, columns].reshape(rows, BLOCK).astype(jnp.float32)

    for hop in range(stat_hops):
        distance = stat_hops - hop
        parts = [stat_block(distance)]
        parts.append(parts[0] if hop == 0 else stat_block(ny - distance))
        for sub in range(SUBS):
            part = slice(sub * sub_rows, (sub + 1) * sub_rows)
            for way in range(2):
                if sub in stat_subs(way, hop):
                    value = parts[way][part]
                    if hop > 0 and sub in stat_subs(way, hop - 1):
                        stat_copy(way, hop - 1, sub).wait_recv()
                        value = value + str_[way, hop - 1, part, :].astype(jnp.float32)
                    sts[way, hop, part, :] = value.astype(jnp.bfloat16)
                    stat_copy(way, hop, sub).start()
    own_part = stat_block(0)
    total_y.wait_recv()
    tzb[z] = total_of(tyb, ny)
    total_z.start()
    pulls = Copies(
        [
            remote(pbs.at[offset], pbr.at[z], pb_sems[0].at[offset - 1], pb_sems[1].at[offset - 1], at_z(offset))
            for offset in range(1, nz)
        ]
    )
    pulls.start()
    total_z.wait_recv()
    terms = float(ny * nz * BLOCK)
    teb[era] = jnp.log(terms) - jnp.log(total_of(tzb, nz) + terms)
    total_era.start()
    total_era.wait_recv()
    for index in range(ne):
        for period in range(years):
            cmat[index * years + period : index * years + period + 1, :] = teb[index, :, period * k : (period + 1) * k]
    cturn[...] = jnp.transpose(cmat[...])

    for sub in range(SUBS):
        part = slice(sub * sub_rows, (sub + 1) * sub_rows)
        value = own_part[part]
        for way in range(2):
            if sub in stat_subs(way, stat_hops - 1):
                stat_copy(way, stat_hops - 1, sub).wait_recv()
                value = value + str_[way, stat_hops - 1, part, :].astype(jnp.float32)
        expo[part, :] = value
    for peer in range(ne):
        for period in range(years):
            start = period * k + peer * slice_rows
            es[peer, period] = expo[start : start + slice_rows, :].astype(jnp.bfloat16)

    def slice_of(offset):
        return pl.ds(pl.multiple_of(lax.rem(era + offset, ne) * slice_rows, slice_rows), slice_rows)

    own_slice = slice_of(0)
    levels = Copies(
        [
            remote(
                es.at[lax.rem(era + offset, ne)],
                er.at[era],
                es_sems[0].at[offset - 1],
                es_sems[1].at[offset - 1],
                at_era(offset),
            )
            for offset in range(1, ne)
        ]
    )
    levels.start()
    er[era] = es[era]
    columns = cturn[own_slice, :]

    def column(index):
        return jnp.broadcast_to(columns[:, index : index + 1], (slice_rows, BLOCK))

    spread = column(all_years)
    noise_scale = column(all_years + 1)
    pulls.wait_recv()
    new_ref[...] = (scale[...] * total_of(pbr, nz)).astype(jnp.bfloat16)
    levels.wait_recv()

    variance = jnp.full((slice_rows, BLOCK), PRIOR_VARIANCE, jnp.float32)
    mean = jnp.zeros((slice_rows, BLOCK), jnp.float32)
    means, weights = [], []
    for period in range(all_years):
        level = jnp.log(er[period // years, period % years].astype(jnp.float32) + 1.0)
        observed = level + column(period)
        noise = noise_scale / (1.0 + level)
        predicted = variance + spread
        gain = predicted / (predicted + noise)
        mean = mean + gain * (observed - mean)
        variance = gain * noise
        means.append(mean)
        weights.append(variance / (variance + spread))
    smooth = means[-1]
    sm[ne - 1, years - 1] = smooth.astype(sm.dtype)
    for period in range(all_years - 2, -1, -1):
        smooth = means[period] + weights[period] * (smooth - means[period])
        sm[period // years, period % years] = smooth.astype(sm.dtype)

    keep = pltpu.make_async_copy(sm.at[era], out_ref.at[:, own_slice], local_sem)
    keep.start()
    results = Copies(
        [
            remote(
                sm.at[lax.rem(era + offset, ne)],
                out_ref.at[:, own_slice],
                out_sems[0].at[offset - 1],
                out_sems[1].at[offset - 1],
                at_era(offset),
            )
            for offset in range(1, ne)
        ]
    )
    results.start()
    for sent in (norm_z, meta, norm_y, words, total_y, total_z, total_era, pulls, levels):
        sent.wait_send()
    for hop in range(hops):
        for item in range(items):
            for way in range(2):
                if item in ring_items(way, hop):
                    ring_copy(way, hop, item).wait_send()
    for hop in range(stat_hops):
        for sub in range(SUBS):
            for way in range(2):
                if sub in stat_subs(way, hop):
                    stat_copy(way, hop, sub).wait_send()
    keep.wait()
    results.wait_send()
    results.wait_recv()


def body(counts, block_term, doc_year, doc_topics, log_params, drift, obs_noise):
    ne = lax.axis_size("era")
    nz = NZ
    ny = lax.axis_size("dp") // nz
    years, k, _ = log_params.shape
    rows = years * k
    nblk = counts.shape[0]
    pieces = next(count for count in (5, 3, 2, 1) if nblk % count == 0)
    sizes = (ne, ny, nz, years, k, nblk, pieces)
    bf16, f32, i32 = jnp.bfloat16, jnp.float32, jnp.int32
    hops = nz // 2
    hbm = pl.BlockSpec(memory_space=pltpu.HBM)
    operands = (
        block_term,
        doc_year,
        counts,
        doc_topics,
        log_params,
        drift.reshape(1, -1),
        obs_noise.reshape(1, -1),
    )
    landing = [
        (pltpu.SMEM if index < 2 else pltpu.VMEM)(value.shape, value.dtype) for index, value in enumerate(operands)
    ]
    slots = [pltpu.VMEM((BLOCK, k), bf16)] * nz + [pltpu.VMEM((nblk + 1, BLOCK, BLOCK), bf16)] * nz
    work = [
        pltpu.VMEM((nz, 8, BLOCK), i32),
        pltpu.SMEM((nz, 8, BLOCK), i32),
        pltpu.VMEM((rows, BLOCK), f32),
        pltpu.VMEM((years, k, ny * BLOCK), bf16),
        pltpu.VMEM((nz, 1, rows), f32),
        pltpu.VMEM((ny, 1, rows), f32),
        pltpu.VMEM((BLOCK, k), f32),
        pltpu.VMEM((rows, nz * BLOCK), bf16),
        pltpu.VMEM((nz * BLOCK, ny * BLOCK), bf16),
        pltpu.VMEM((nz, BLOCK, k), bf16),
        pltpu.VMEM((nz, BLOCK, k), bf16),
        pltpu.VMEM((2, ny // 2, rows, BLOCK), bf16),
        pltpu.VMEM((2, ny // 2, rows, BLOCK), bf16),
        pltpu.VMEM((ny, 1, rows), f32),
        pltpu.VMEM((nz, 1, rows), f32),
        pltpu.VMEM((ne, 1, rows), f32),
        pltpu.VMEM((BLOCK, k), f32),
        pltpu.VMEM((k, BLOCK), f32),
        pltpu.VMEM((ne, years, k // ne, BLOCK), bf16),
        pltpu.VMEM((ne, years, k // ne, BLOCK), bf16),
        pltpu.VMEM((ne, years, k // ne, BLOCK), bf16),
    ]
    dma = pltpu.SemaphoreType.DMA
    ring_sems = dma((2, hops, pieces + 1))
    sems = [dma((len(operands),)), ring_sems, ring_sems, dma]
    for count in (nz, ny, nz, ny, nz, 0, ny, nz, ne, ne, ne):
        sems += [dma((count - 1,)) if count else dma((2, ny // 2, SUBS))] * 2
    new_topics, smoothed = pl.pallas_call(
        functools.partial(kernel, sizes),
        out_shape=(
            jax.ShapeDtypeStruct(doc_topics.shape, bf16),
            jax.ShapeDtypeStruct(log_params.shape, bf16),
        ),
        in_specs=[hbm] * len(operands),
        out_specs=(pl.BlockSpec(memory_space=pltpu.VMEM), pl.BlockSpec(memory_space=pl.ANY)),
        scratch_shapes=landing + slots + work + sems,
        compiler_params=pltpu.CompilerParams(
            collective_id=0, has_side_effects=True, vmem_limit_bytes=60 * 1024 * 1024
        ),
    )(*operands)
    return (new_topics, smoothed.astype(f32))


def solution(mesh):
    return jax.shard_map(
        body,
        mesh=mesh,
        in_specs=(
            P(("era", "dp"), None, None),
            P(("era", "dp")),
            P(("era", "dp")),
            P(("era", "dp"), None),
            P("era", None, "dp"),
            P(),
            P(),
        ),
        out_specs=(P(("era", "dp"), None), P("era", None, "dp")),
        check_vma=False,
    )
```

```python
import functools

import jax
import jax.numpy as jnp
from jax import lax
from jax.experimental import pallas as pl
from jax.experimental.pallas import tpu as pltpu
from jax.sharding import PartitionSpec as P

MESH = pl.DeviceIdType.MESH
NZ = 8
PRIOR_VARIANCE = 1.0
BLOCK = 128
SUBS = 4


def dot(a, b, contract):
    return lax.dot_general(a, b, (contract, ((), ())), preferred_element_type=jnp.float32)


def row_sums(value):
    return jnp.sum(jnp.transpose(value), axis=0, keepdims=True)


class Copies:
    def __init__(self, copies):
        self.copies = copies

    def start(self):
        for copy in self.copies:
            copy.start()

    def wait_recv(self):
        for copy in self.copies:
            copy.wait_recv()

    def wait_send(self):
        for copy in self.copies:
            copy.wait_send()


def remote(src, dst, send_sem, recv_sem, device):
    return pltpu.make_async_remote_copy(
        src_ref=src, dst_ref=dst, send_sem=send_sem, recv_sem=recv_sem, device_id=device, device_id_type=MESH
    )


def kernel(sizes, *refs):
    ne, ny, nz, years, k, nblk, pieces = sizes
    refs = list(refs)

    def take(count=None):
        if count is None:
            return refs.pop(0)
        return [refs.pop(0) for _ in range(count)]

    bterm_in, dyear_in, counts_in, topics_in, logp_in, drift_in, onoise_in = take(7)
    new_ref, out_ref = take(2)
    bterm, dyear, counts, topics, logp, drift, onoise = take(7)
    low = take(nz)
    cnt = take(nz)
    mbuf, msmem, expo, wbuf, nzb, nyb, scale, ptall, rall = take(9)
    pbs, pbr, sts, str_, tyb, tzb, teb, cmat, cturn, es, er, sm = take(12)
    in_sems, ring_send, ring_recv, local_sem = take(4)
    pairs = [take(2) for _ in range(len(refs) // 2)]
    m_sems, w_sems, nz_sems, ny_sems, pb_sems, st_sems, ty_sems, tz_sems, te_sems, es_sems, out_sems = pairs

    rows = years * k
    all_years = ne * years
    slice_rows = k // ne
    era = lax.axis_index("era")
    dp = lax.axis_index("dp")
    y = dp // nz
    z = lax.rem(dp, nz)

    def at_z(offset):
        return {"dp": y * nz + lax.rem(z + offset, nz)}

    def at_y(offset):
        return {"dp": lax.rem(y + offset, ny) * nz + z}

    def at_era(offset):
        return {"era": lax.rem(era + offset, ne)}

    def spread_out(buffer, me, count, target, sems):
        send, recv = sems
        return Copies(
            [
                remote(buffer.at[me], buffer.at[me], send.at[offset - 1], recv.at[offset - 1], target(offset))
                for offset in range(1, count)
            ]
        )

    def total_of(buffer, count):
        total = buffer[0].astype(jnp.float32)
        for slot in range(1, count):
            total = total + buffer[slot].astype(jnp.float32)
        return total

    barrier = pltpu.get_barrier_semaphore()
    for target, count in ((at_z, nz), (at_y, ny), (at_era, ne)):
        for offset in range(1, count):
            pl.semaphore_signal(barrier, inc=1, device_id=target(offset), device_id_type=MESH)
    inputs = (
        (logp_in, logp),
        (topics_in, topics),
        (counts_in, counts),
        (bterm_in, bterm),
        (dyear_in, dyear),
        (drift_in, drift),
        (onoise_in, onoise),
    )
    loads = [pltpu.make_async_copy(src, dst, in_sems.at[index]) for index, (src, dst) in enumerate(inputs)]
    for load in loads:
        load.start()

    loads[0].wait()
    exponent = jnp.exp(logp[...].reshape(rows, BLOCK))
    expo[...] = exponent
    nzb[z] = row_sums(exponent)
    loads[1].wait()
    proportion = topics[...].astype(jnp.float32)
    proportion = proportion / jnp.sum(proportion, axis=1, keepdims=True)
    low[0][...] = proportion.astype(jnp.bfloat16)
    for load in loads[3:]:
        load.wait()
    lane = lax.broadcasted_iota(jnp.int32, (8, BLOCK), 1)
    place = jnp.full((8, BLOCK), nblk, jnp.int32)
    for index in range(nblk):
        place = jnp.where(lane == bterm[index], index, place)
    place = jnp.where(lane == ny * nz, lax.rem(dyear[0], years), place)
    mbuf[z] = place
    loads[2].wait()

    norm_z = spread_out(nzb, z, nz, at_z, nz_sems)
    norm_y = spread_out(nyb, y, ny, at_y, ny_sems)
    meta = spread_out(mbuf, z, nz, at_z, m_sems)

    per_piece = nblk // pieces
    hops = nz // 2
    items = pieces + 1

    def ring_items(way, hop):
        if hop < hops - 1:
            return list(range(items))
        return list(range(items // 2)) if way == 0 else list(range(items // 2, items))

    def ring_copy(way, hop, item):
        here = hop if way else (nz - hop) % nz
        there = hop + 1 if way else nz - hop - 1
        if item == 0:
            src, dst = low[here], low[there]
        else:
            block = pl.ds((item - 1) * per_piece, per_piece)
            src, dst = cnt[here].at[block], cnt[there].at[block]
        return remote(
            src, dst, ring_send.at[way, hop, item], ring_recv.at[way, hop, item], at_z(nz - 1 if way else 1)
        )

    def ring_pass(hop, which):
        for item in which:
            for way in range(2):
                if item in ring_items(way, hop):
                    ring_copy(way, hop, item).wait_recv()
                    if hop + 1 < hops and item in ring_items(way, hop + 1):
                        ring_copy(way, hop + 1, item).start()

    length = jnp.zeros((BLOCK, BLOCK), jnp.int32)
    for index in range(nblk):
        value = counts[index]
        length = length + value
        cnt[0][index] = value.astype(jnp.float32).astype(jnp.bfloat16)
    pl.semaphore_wait(barrier, nz + ny + ne - 3)
    norm_z.start()
    for item in range(items):
        for way in range(2):
            if item in ring_items(way, 0):
                ring_copy(way, 0, item).start()
    meta.start()
    for slot in range(nz):
        cnt[slot][nblk] = jnp.zeros((BLOCK, BLOCK), jnp.bfloat16)
    doc_length = jnp.sum(length.astype(jnp.float32), axis=1, keepdims=True)
    scale[...] = float(k) * proportion / doc_length
    cmat[...] = jnp.zeros_like(cmat)
    cmat[all_years : all_years + 1, :] = drift[...]
    cmat[all_years + 1 : all_years + 2, :] = onoise[...]

    norm_z.wait_recv()
    nyb[y] = total_of(nzb, nz)
    norm_y.start()
    norm_y.wait_recv()
    normalizer = jnp.transpose(jnp.broadcast_to(total_of(nyb, ny), (BLOCK, rows)))
    own_columns = pl.ds(pl.multiple_of(y * BLOCK, BLOCK), BLOCK)
    wbuf[:, :, own_columns] = (expo[...] / normalizer).astype(jnp.bfloat16).reshape(years, k, BLOCK)
    own_words = wbuf.at[:, :, own_columns]
    words = Copies(
        [
            remote(own_words, own_words, w_sems[0].at[offset - 1], w_sems[1].at[offset - 1], at_y(offset))
            for offset in range(1, ny)
        ]
    )
    words.start()

    totals = [jnp.zeros((1, k), jnp.float32) for _ in range(years)]

    def document_block(slot):
        source = lax.rem(z + slot, nz)
        year = msmem[source, 0, ny * nz]
        left = low[slot][...]
        table = wbuf[year]
        scores = dot(left, table, ((1,), (0,)))
        here = slice(slot * BLOCK, (slot + 1) * BLOCK)
        for column in range(ny):
            block = cnt[slot][msmem[source, 0, column * nz + z]].astype(jnp.float32)
            terms = slice(column * BLOCK, (column + 1) * BLOCK)
            rall[here, terms] = (block / scores[:, terms]).astype(jnp.bfloat16)
        pull = dot(rall[here, :], table, ((1,), (1,)))
        left = left.astype(jnp.float32)
        share = jnp.sum(left * pull, axis=0, keepdims=True)
        turned = jnp.transpose(left)
        for period in range(years):
            flag = (year == period).astype(jnp.float32)
            ptall[period * k : (period + 1) * k, here] = (turned * flag).astype(jnp.bfloat16)
            totals[period] = totals[period] + share * flag
        if slot == 0:
            pbr[z] = pull.astype(jnp.bfloat16)
        else:
            pbs[slot] = pull.astype(jnp.bfloat16)

    order = [0]
    for step in range(1, hops):
        order += [step, nz - step]
    order.append(hops)
    done = 0
    for hop in range(hops):
        last = hop == hops - 2 or hops == 1
        if last:
            ring_pass(hop, range(items // 2))
            words.wait_recv()
            meta.wait_recv()
            to_smem = pltpu.make_async_copy(mbuf, msmem, local_sem)
            to_smem.start()
            to_smem.wait()
            while done < min(3, 2 * hop + 1):
                document_block(order[done])
                done += 1
            ring_pass(hop, range(items // 2, items))
        else:
            ring_pass(hop, range(0 if hop == 0 else 0, items))
        if hop >= hops - 2:
            ready = nz if hop == hops - 1 else 2 * hop + 3
            while done < ready:
                document_block(order[done])
                done += 1

    tyb[y] = jnp.concatenate(totals, axis=1)
    total_y = spread_out(tyb, y, ny, at_y, ty_sems)
    total_z = spread_out(tzb, z, nz, at_z, tz_sems)
    total_era = spread_out(teb, era, ne, at_era, te_sems)
    total_y.start()

    stat_hops = ny // 2
    sub_rows = rows // SUBS

    def stat_subs(way, hop):
        if hop > 0:
            return list(range(SUBS))
        return list(range(SUBS // 2)) if way == 0 else list(range(SUBS // 2, SUBS))

    def stat_copy(way, hop, sub):
        part = pl.ds(sub * sub_rows, sub_rows)
        return remote(
            sts.at[way, hop, part],
            str_.at[way, hop, part],
            st_sems[0].at[way, hop, sub],
            st_sems[1].at[way, hop, sub],
            at_y(ny - 1 if way else 1),
        )

    def stat_block(offset):
        columns = pl.ds(pl.multiple_of(lax.rem(y + offset, ny) * BLOCK, BLOCK), BLOCK)
        part = dot(ptall[...], rall[:, columns], ((1,), (0,)))
        return part * wbuf[:, :, columns].reshape(rows, BLOCK).astype(jnp.float32)

    terms = float(ny * nz * BLOCK)
    pulls = Copies(
        [
            remote(pbs.at[offset], pbr.at[z], pb_sems[0].at[offset - 1], pb_sems[1].at[offset - 1], at_z(offset))
            for offset in range(1, nz)
        ]
    )

    def after_y():
        total_y.wait_recv()
        tzb[z] = total_of(tyb, ny)
        total_z.start()

    def after_z():
        total_z.wait_recv()
        teb[era] = jnp.log(terms) - jnp.log(total_of(tzb, nz) + terms)
        total_era.start()
        pulls.start()

    def after_era():
        total_era.wait_recv()
        for index in range(ne):
            for period in range(years):
                line = index * years + period
                cmat[line : line + 1, :] = teb[index, :, period * k : (period + 1) * k]
        cturn[...] = jnp.transpose(cmat[...])

    beside = [after_y, after_z, after_era]
    for hop in range(stat_hops):
        distance = stat_hops - hop
        parts = [stat_block(distance)]
        parts.append(parts[0] if hop == 0 else stat_block(ny - distance))
        if hop > 0 and beside:
            beside.pop(0)()
        for sub in range(SUBS):
            part = slice(sub * sub_rows, (sub + 1) * sub_rows)
            for way in range(2):
                if sub in stat_subs(way, hop):
                    value = parts[way][part]
                    if hop > 0 and sub in stat_subs(way, hop - 1):
                        stat_copy(way, hop - 1, sub).wait_recv()
                        value = value + str_[way, hop - 1, part, :].astype(jnp.float32)
                    sts[way, hop, part, :] = value.astype(jnp.bfloat16)
                    stat_copy(way, hop, sub).start()
    own_part = stat_block(0)
    for step in beside:
        step()

    for sub in range(SUBS):
        part = slice(sub * sub_rows, (sub + 1) * sub_rows)
        value = own_part[part]
        for way in range(2):
            if sub in stat_subs(way, stat_hops - 1):
                stat_copy(way, stat_hops - 1, sub).wait_recv()
                value = value + str_[way, stat_hops - 1, part, :].astype(jnp.float32)
        expo[part, :] = value
    for peer in range(ne):
        for period in range(years):
            start = period * k + peer * slice_rows
            es[peer, period] = expo[start : start + slice_rows, :].astype(jnp.bfloat16)

    def slice_of(offset):
        return pl.ds(pl.multiple_of(lax.rem(era + offset, ne) * slice_rows, slice_rows), slice_rows)

    own_slice = slice_of(0)
    levels = Copies(
        [
            remote(
                es.at[lax.rem(era + offset, ne)],
                er.at[era],
                es_sems[0].at[offset - 1],
                es_sems[1].at[offset - 1],
                at_era(offset),
            )
            for offset in range(1, ne)
        ]
    )
    levels.start()
    er[era] = es[era]
    columns = cturn[own_slice, :]

    def column(index):
        return jnp.broadcast_to(columns[:, index : index + 1], (slice_rows, BLOCK))

    spread = column(all_years)
    noise_scale = column(all_years + 1)
    levels.wait_recv()

    variance = jnp.full((slice_rows, BLOCK), PRIOR_VARIANCE, jnp.float32)
    mean = jnp.zeros((slice_rows, BLOCK), jnp.float32)
    means, weights = [], []
    for period in range(all_years):
        level = jnp.log(er[period // years, period % years].astype(jnp.float32) + 1.0)
        observed = level + column(period)
        noise = noise_scale / (1.0 + level)
        predicted = variance + spread
        gain = predicted / (predicted + noise)
        mean = mean + gain * (observed - mean)
        variance = gain * noise
        means.append(mean)
        weights.append(variance / (variance + spread))
    smooth = means[-1]
    sm[ne - 1, years - 1] = smooth.astype(sm.dtype)
    for period in range(all_years - 2, -1, -1):
        smooth = means[period] + weights[period] * (smooth - means[period])
        sm[period // years, period % years] = smooth.astype(sm.dtype)

    keep = pltpu.make_async_copy(sm.at[era], out_ref.at[:, own_slice], local_sem)
    keep.start()
    results = Copies(
        [
            remote(
                sm.at[lax.rem(era + offset, ne)],
                out_ref.at[:, own_slice],
                out_sems[0].at[offset - 1],
                out_sems[1].at[offset - 1],
                at_era(offset),
            )
            for offset in range(1, ne)
        ]
    )
    results.start()
    pulls.wait_recv()
    new_ref[...] = (scale[...] * total_of(pbr, nz)).astype(jnp.bfloat16)
    for sent in (norm_z, meta, norm_y, words, total_y, total_z, total_era, pulls, levels):
        sent.wait_send()
    for hop in range(hops):
        for item in range(items):
            for way in range(2):
                if item in ring_items(way, hop):
                    ring_copy(way, hop, item).wait_send()
    for hop in range(stat_hops):
        for sub in range(SUBS):
            for way in range(2):
                if sub in stat_subs(way, hop):
                    stat_copy(way, hop, sub).wait_send()
    keep.wait()
    results.wait_send()
    results.wait_recv()


def body(counts, block_term, doc_year, doc_topics, log_params, drift, obs_noise):
    ne = lax.axis_size("era")
    nz = NZ
    ny = lax.axis_size("dp") // nz
    years, k, _ = log_params.shape
    rows = years * k
    nblk = counts.shape[0]
    pieces = next(count for count in (5, 3, 2, 1) if nblk % count == 0)
    sizes = (ne, ny, nz, years, k, nblk, pieces)
    bf16, f32, i32 = jnp.bfloat16, jnp.float32, jnp.int32
    hops = nz // 2
    hbm = pl.BlockSpec(memory_space=pltpu.HBM)
    operands = (
        block_term,
        doc_year,
        counts,
        doc_topics,
        log_params,
        drift.reshape(1, -1),
        obs_noise.reshape(1, -1),
    )
    landing = [
        (pltpu.SMEM if index < 2 else pltpu.VMEM)(value.shape, value.dtype) for index, value in enumerate(operands)
    ]
    slots = [pltpu.VMEM((BLOCK, k), bf16)] * nz + [pltpu.VMEM((nblk + 1, BLOCK, BLOCK), bf16)] * nz
    work = [
        pltpu.VMEM((nz, 8, BLOCK), i32),
        pltpu.SMEM((nz, 8, BLOCK), i32),
        pltpu.VMEM((rows, BLOCK), f32),
        pltpu.VMEM((years, k, ny * BLOCK), bf16),
        pltpu.VMEM((nz, 1, rows), f32),
        pltpu.VMEM((ny, 1, rows), f32),
        pltpu.VMEM((BLOCK, k), f32),
        pltpu.VMEM((rows, nz * BLOCK), bf16),
        pltpu.VMEM((nz * BLOCK, ny * BLOCK), bf16),
        pltpu.VMEM((nz, BLOCK, k), bf16),
        pltpu.VMEM((nz, BLOCK, k), bf16),
        pltpu.VMEM((2, ny // 2, rows, BLOCK), bf16),
        pltpu.VMEM((2, ny // 2, rows, BLOCK), bf16),
        pltpu.VMEM((ny, 1, rows), f32),
        pltpu.VMEM((nz, 1, rows), f32),
        pltpu.VMEM((ne, 1, rows), f32),
        pltpu.VMEM((BLOCK, k), f32),
        pltpu.VMEM((k, BLOCK), f32),
        pltpu.VMEM((ne, years, k // ne, BLOCK), bf16),
        pltpu.VMEM((ne, years, k // ne, BLOCK), bf16),
        pltpu.VMEM((ne, years, k // ne, BLOCK), bf16),
    ]
    dma = pltpu.SemaphoreType.DMA
    ring_sems = dma((2, hops, pieces + 1))
    sems = [dma((len(operands),)), ring_sems, ring_sems, dma]
    for count in (nz, ny, nz, ny, nz, 0, ny, nz, ne, ne, ne):
        sems += [dma((count - 1,)) if count else dma((2, ny // 2, SUBS))] * 2
    new_topics, smoothed = pl.pallas_call(
        functools.partial(kernel, sizes),
        out_shape=(
            jax.ShapeDtypeStruct(doc_topics.shape, bf16),
            jax.ShapeDtypeStruct(log_params.shape, bf16),
        ),
        in_specs=[hbm] * len(operands),
        out_specs=(pl.BlockSpec(memory_space=pltpu.VMEM), pl.BlockSpec(memory_space=pl.ANY)),
        scratch_shapes=landing + slots + work + sems,
        compiler_params=pltpu.CompilerParams(
            collective_id=0, has_side_effects=True, vmem_limit_bytes=60 * 1024 * 1024
        ),
    )(*operands)
    return (new_topics, smoothed.astype(f32))


def solution(mesh):
    return jax.shard_map(
        body,
        mesh=mesh,
        in_specs=(
            P(("era", "dp"), None, None),
            P(("era", "dp")),
            P(("era", "dp")),
            P(("era", "dp"), None),
            P("era", None, "dp"),
            P(),
            P(),
        ),
        out_specs=(P(("era", "dp"), None), P("era", None, "dp")),
        check_vma=False,
    )
```

```python
import functools

import jax
import jax.numpy as jnp
from jax import lax
from jax.experimental import pallas as pl
from jax.experimental.pallas import tpu as pltpu
from jax.sharding import PartitionSpec as P

MESH = pl.DeviceIdType.MESH
NZ = 8
PRIOR_VARIANCE = 1.0
BLOCK = 128
SUBS = 4
LARGEST_PIECE = 4


def dot(a, b, contract):
    return lax.dot_general(a, b, (contract, ((), ())), preferred_element_type=jnp.float32)


def row_sums(value):
    return jnp.sum(jnp.transpose(value), axis=0, keepdims=True)


class Copies:
    def __init__(self, copies):
        self.copies = copies

    def start(self):
        for copy in self.copies:
            copy.start()

    def wait_recv(self):
        for copy in self.copies:
            copy.wait_recv()

    def wait_send(self):
        for copy in self.copies:
            copy.wait_send()


def remote(src, dst, send_sem, recv_sem, device):
    return pltpu.make_async_remote_copy(
        src_ref=src, dst_ref=dst, send_sem=send_sem, recv_sem=recv_sem, device_id=device, device_id_type=MESH
    )


def blocks_needed(way, hop, ny, nz, nblk):
    half = ny - ny // 2 if way else ny // 2
    return min(nblk, half + ny * (nz // 2 - 1 - hop))


def ring_pieces(way, ny, nz, nblk):
    ends = sorted({blocks_needed(way, hop, ny, nz, nblk) for hop in range(nz // 2)} | {nblk})
    parts, start = [], 0
    for end in ends:
        while start < end:
            stop = min(end, start + LARGEST_PIECE)
            parts.append((start, stop))
            start = stop
    return parts


def kernel(sizes, *refs):
    ne, ny, nz, years, k, nblk, pieces = sizes
    refs = list(refs)

    def take(count=None):
        if count is None:
            return refs.pop(0)
        return [refs.pop(0) for _ in range(count)]

    bterm_in, dyear_in, counts_in, topics_in, logp_in, drift_in, onoise_in = take(7)
    new_ref, out_ref = take(2)
    bterm, dyear, counts, topics, logp, drift, onoise = take(7)
    low = take(nz)
    cnt = take(nz)
    mbuf, msmem, expo, wbuf, nzb, nyb, scale, ptall, rall = take(9)
    pbs, pbr, sts, str_, tyb, tzb, teb, cmat, cturn, es, er, sm = take(12)
    in_sems, ring_send, ring_recv, local_sem = take(4)
    pairs = [take(2) for _ in range(len(refs) // 2)]
    m_sems, w_sems, nz_sems, ny_sems, pb_sems, st_sems, ty_sems, tz_sems, te_sems, es_sems, out_sems = pairs

    rows = years * k
    all_years = ne * years
    slice_rows = k // ne
    era = lax.axis_index("era")
    dp = lax.axis_index("dp")
    y = dp // nz
    z = lax.rem(dp, nz)

    def at_z(offset):
        return {"dp": y * nz + lax.rem(z + offset, nz)}

    def at_y(offset):
        return {"dp": lax.rem(y + offset, ny) * nz + z}

    def at_era(offset):
        return {"era": lax.rem(era + offset, ne)}

    def spread_out(buffer, me, count, target, sems):
        send, recv = sems
        return Copies(
            [
                remote(buffer.at[me], buffer.at[me], send.at[offset - 1], recv.at[offset - 1], target(offset))
                for offset in range(1, count)
            ]
        )

    def total_of(buffer, count):
        total = buffer[0].astype(jnp.float32)
        for slot in range(1, count):
            total = total + buffer[slot].astype(jnp.float32)
        return total

    barrier = pltpu.get_barrier_semaphore()
    for target, count in ((at_z, nz), (at_y, ny), (at_era, ne)):
        for offset in range(1, count):
            pl.semaphore_signal(barrier, inc=1, device_id=target(offset), device_id_type=MESH)
    inputs = (
        (logp_in, logp),
        (topics_in, topics),
        (counts_in, counts),
        (bterm_in, bterm),
        (dyear_in, dyear),
        (drift_in, drift),
        (onoise_in, onoise),
    )
    loads = [pltpu.make_async_copy(src, dst, in_sems.at[index]) for index, (src, dst) in enumerate(inputs)]
    for load in loads:
        load.start()

    loads[0].wait()
    exponent = jnp.exp(logp[...].reshape(rows, BLOCK))
    expo[...] = exponent
    nzb[z] = row_sums(exponent)
    loads[1].wait()
    proportion = topics[...].astype(jnp.float32)
    proportion = proportion / jnp.sum(proportion, axis=1, keepdims=True)
    low[0][...] = proportion.astype(jnp.bfloat16)

    norm_z = spread_out(nzb, z, nz, at_z, nz_sems)
    norm_y = spread_out(nyb, y, ny, at_y, ny_sems)
    meta = spread_out(mbuf, z, nz, at_z, m_sems)

    hops = nz // 2
    items = 1 + max(len(part) for part in pieces)

    def ring_items(way, hop):
        need = blocks_needed(way, hop, ny, nz, nblk)
        return [0] + [1 + index for index, (_, end) in enumerate(pieces[way]) if end <= need]

    def ring_copy(way, hop, item):
        here = hop if way else (nz - hop) % nz
        there = hop + 1 if way else nz - hop - 1
        if item == 0:
            src, dst = low[here], low[there]
            if hop == hops - 1:
                half = pl.ds(way * (BLOCK // 2), BLOCK // 2)
                src, dst = src.at[half], dst.at[half]
        else:
            start, end = pieces[way][item - 1]
            block = pl.ds(nblk - end if way else start, end - start)
            src, dst = cnt[here].at[block], cnt[there].at[block]
        return remote(
            src, dst, ring_send.at[way, hop, item], ring_recv.at[way, hop, item], at_z(nz - 1 if way else 1)
        )

    def ring_pass(hop, which):
        for item in which:
            for way in range(2):
                if item in ring_items(way, hop):
                    ring_copy(way, hop, item).wait_recv()
                    if hop + 1 < hops and item in ring_items(way, hop + 1):
                        ring_copy(way, hop + 1, item).start()

    pl.semaphore_wait(barrier, nz + ny + ne - 3)
    norm_z.start()
    for way in range(2):
        ring_copy(way, 0, 0).start()

    for load in loads[2:]:
        load.wait()
    keys, antipodal = [], 0
    for index in range(nblk):
        distance = lax.rem(lax.rem(bterm[index], nz) - z + nz, nz)
        opposite = distance == hops
        key = jnp.where(distance < hops, -distance, nz - distance)
        keys.append(jnp.where(opposite, jnp.where(antipodal < ny // 2, -hops, hops), key))
        antipodal = antipodal + jnp.where(opposite, 1, 0)
    position = [0] * nblk
    for later in range(nblk):
        for earlier in range(later):
            before = jnp.where(keys[earlier] <= keys[later], 1, 0)
            position[later] = position[later] + before
            position[earlier] = position[earlier] + (1 - before)
    length = jnp.zeros((BLOCK, BLOCK), jnp.int32)
    filled = set()
    for step in range(max(len(part) for part in pieces)):
        for way in range(2):
            if step < len(pieces[way]):
                start, end = pieces[way][step]
                if way:
                    start, end = nblk - end, nblk - start
                for place in range(start, end):
                    if place not in filled:
                        filled.add(place)
                        block = sum(jnp.where(position[index] == place, index, 0) for index in range(nblk))
                        value = counts[block]
                        length = length + value
                        cnt[0][place] = value.astype(jnp.float32).astype(jnp.bfloat16)
                if 1 + step in ring_items(way, 0):
                    ring_copy(way, 0, 1 + step).start()
    lane = lax.broadcasted_iota(jnp.int32, (8, BLOCK), 1)
    table = jnp.full((8, BLOCK), nblk, jnp.int32)
    for index in range(nblk):
        table = jnp.where(lane == bterm[index], position[index], table)
    table = jnp.where(lane == ny * nz, lax.rem(dyear[0], years), table)
    mbuf[z] = table
    meta.start()
    for slot in range(nz):
        cnt[slot][nblk] = jnp.zeros((BLOCK, BLOCK), jnp.bfloat16)
    doc_length = jnp.sum(length.astype(jnp.float32), axis=1, keepdims=True)
    scale[...] = float(k) * proportion / doc_length
    cmat[...] = jnp.zeros_like(cmat)
    cmat[all_years : all_years + 1, :] = drift[...]
    cmat[all_years + 1 : all_years + 2, :] = onoise[...]

    norm_z.wait_recv()
    nyb[y] = total_of(nzb, nz)
    norm_y.start()
    norm_y.wait_recv()
    normalizer = jnp.transpose(jnp.broadcast_to(total_of(nyb, ny), (BLOCK, rows)))
    own_columns = pl.ds(pl.multiple_of(y * BLOCK, BLOCK), BLOCK)
    wbuf[:, :, own_columns] = (expo[...] / normalizer).astype(jnp.bfloat16).reshape(years, k, BLOCK)
    own_words = wbuf.at[:, :, own_columns]
    words = Copies(
        [
            remote(own_words, own_words, w_sems[0].at[offset - 1], w_sems[1].at[offset - 1], at_y(offset))
            for offset in range(1, ny)
        ]
    )
    words.start()

    totals = [jnp.zeros((1, k), jnp.float32) for _ in range(years)]

    def document_block(slot):
        source = lax.rem(z + slot, nz)
        year = msmem[source, 0, ny * nz]
        left = low[slot][...]
        table = wbuf[year]
        scores = dot(left, table, ((1,), (0,)))
        here = slice(slot * BLOCK, (slot + 1) * BLOCK)
        for column in range(ny):
            block = cnt[slot][msmem[source, 0, column * nz + z]].astype(jnp.float32)
            terms = slice(column * BLOCK, (column + 1) * BLOCK)
            rall[here, terms] = (block / scores[:, terms]).astype(jnp.bfloat16)
        pull = dot(rall[here, :], table, ((1,), (1,)))
        left = left.astype(jnp.float32)
        share = jnp.sum(left * pull, axis=0, keepdims=True)
        turned = jnp.transpose(left)
        for period in range(years):
            flag = (year == period).astype(jnp.float32)
            ptall[period * k : (period + 1) * k, here] = (turned * flag).astype(jnp.bfloat16)
            totals[period] = totals[period] + share * flag
        if slot == 0:
            pbr[z] = pull.astype(jnp.bfloat16)
        else:
            pbs[slot] = pull.astype(jnp.bfloat16)

    order = [0]
    for step in range(1, hops):
        order += [step, nz - step]
    order.append(hops)
    done = 0
    for hop in range(hops):
        last = hop == hops - 2 or hops == 1
        if last:
            ring_pass(hop, range(items // 2))
            words.wait_recv()
            meta.wait_recv()
            to_smem = pltpu.make_async_copy(mbuf, msmem, local_sem)
            to_smem.start()
            to_smem.wait()
            while done < min(3, 2 * hop + 1):
                document_block(order[done])
                done += 1
            ring_pass(hop, range(items // 2, items))
        else:
            ring_pass(hop, range(0 if hop == 0 else 0, items))
        if hop >= hops - 2:
            ready = nz if hop == hops - 1 else 2 * hop + 3
            while done < ready:
                document_block(order[done])
                done += 1

    tyb[y] = jnp.concatenate(totals, axis=1)
    total_y = spread_out(tyb, y, ny, at_y, ty_sems)
    total_z = spread_out(tzb, z, nz, at_z, tz_sems)
    total_era = spread_out(teb, era, ne, at_era, te_sems)
    total_y.start()

    stat_hops = ny // 2
    sub_rows = rows // SUBS

    def stat_subs(way, hop):
        if hop > 0:
            return list(range(SUBS))
        return list(range(SUBS // 2)) if way == 0 else list(range(SUBS // 2, SUBS))

    def stat_copy(way, hop, sub):
        part = pl.ds(sub * sub_rows, sub_rows)
        return remote(
            sts.at[way, hop, part],
            str_.at[way, hop, part],
            st_sems[0].at[way, hop, sub],
            st_sems[1].at[way, hop, sub],
            at_y(ny - 1 if way else 1),
        )

    def stat_block(offset):
        columns = pl.ds(pl.multiple_of(lax.rem(y + offset, ny) * BLOCK, BLOCK), BLOCK)
        part = dot(ptall[...], rall[:, columns], ((1,), (0,)))
        return part * wbuf[:, :, columns].reshape(rows, BLOCK).astype(jnp.float32)

    terms = float(ny * nz * BLOCK)
    pulls = Copies(
        [
            remote(pbs.at[offset], pbr.at[z], pb_sems[0].at[offset - 1], pb_sems[1].at[offset - 1], at_z(offset))
            for offset in range(1, nz)
        ]
    )

    def after_y():
        total_y.wait_recv()
        tzb[z] = total_of(tyb, ny)
        total_z.start()

    def after_z():
        total_z.wait_recv()
        teb[era] = jnp.log(terms) - jnp.log(total_of(tzb, nz) + terms)
        total_era.start()
        pulls.start()

    def after_era():
        total_era.wait_recv()
        for index in range(ne):
            for period in range(years):
                line = index * years + period
                cmat[line : line + 1, :] = teb[index, :, period * k : (period + 1) * k]
        cturn[...] = jnp.transpose(cmat[...])

    beside = [after_y, after_z, after_era]
    for hop in range(stat_hops):
        distance = stat_hops - hop
        parts = [stat_block(distance)]
        parts.append(parts[0] if hop == 0 else stat_block(ny - distance))
        if hop > 0 and beside:
            beside.pop(0)()
        for sub in range(SUBS):
            part = slice(sub * sub_rows, (sub + 1) * sub_rows)
            for way in range(2):
                if sub in stat_subs(way, hop):
                    value = parts[way][part]
                    if hop > 0 and sub in stat_subs(way, hop - 1):
                        stat_copy(way, hop - 1, sub).wait_recv()
                        value = value + str_[way, hop - 1, part, :].astype(jnp.float32)
                    sts[way, hop, part, :] = value.astype(jnp.bfloat16)
                    stat_copy(way, hop, sub).start()
    own_part = stat_block(0)
    for step in beside:
        step()

    for sub in range(SUBS):
        part = slice(sub * sub_rows, (sub + 1) * sub_rows)
        value = own_part[part]
        for way in range(2):
            if sub in stat_subs(way, stat_hops - 1):
                stat_copy(way, stat_hops - 1, sub).wait_recv()
                value = value + str_[way, stat_hops - 1, part, :].astype(jnp.float32)
        expo[part, :] = value
    for peer in range(ne):
        for period in range(years):
            start = period * k + peer * slice_rows
            es[peer, period] = expo[start : start + slice_rows, :].astype(jnp.bfloat16)

    def slice_of(offset):
        return pl.ds(pl.multiple_of(lax.rem(era + offset, ne) * slice_rows, slice_rows), slice_rows)

    own_slice = slice_of(0)
    levels = Copies(
        [
            remote(
                es.at[lax.rem(era + offset, ne)],
                er.at[era],
                es_sems[0].at[offset - 1],
                es_sems[1].at[offset - 1],
                at_era(offset),
            )
            for offset in range(1, ne)
        ]
    )
    levels.start()
    er[era] = es[era]
    columns = cturn[own_slice, :]

    def column(index):
        return jnp.broadcast_to(columns[:, index : index + 1], (slice_rows, BLOCK))

    spread = column(all_years)
    noise_scale = column(all_years + 1)
    levels.wait_recv()

    variance = jnp.full((slice_rows, BLOCK), PRIOR_VARIANCE, jnp.float32)
    mean = jnp.zeros((slice_rows, BLOCK), jnp.float32)
    means, weights = [], []
    for period in range(all_years):
        level = jnp.log(er[period // years, period % years].astype(jnp.float32) + 1.0)
        observed = level + column(period)
        noise = noise_scale / (1.0 + level)
        predicted = variance + spread
        gain = predicted / (predicted + noise)
        mean = mean + gain * (observed - mean)
        variance = gain * noise
        means.append(mean)
        weights.append(variance / (variance + spread))
    smooth = means[-1]
    sm[ne - 1, years - 1] = smooth.astype(sm.dtype)
    for period in range(all_years - 2, -1, -1):
        smooth = means[period] + weights[period] * (smooth - means[period])
        sm[period // years, period % years] = smooth.astype(sm.dtype)

    keep = pltpu.make_async_copy(sm.at[era], out_ref.at[:, own_slice], local_sem)
    keep.start()
    results = Copies(
        [
            remote(
                sm.at[lax.rem(era + offset, ne)],
                out_ref.at[:, own_slice],
                out_sems[0].at[offset - 1],
                out_sems[1].at[offset - 1],
                at_era(offset),
            )
            for offset in range(1, ne)
        ]
    )
    results.start()
    pulls.wait_recv()
    new_ref[...] = (scale[...] * total_of(pbr, nz)).astype(jnp.bfloat16)
    for sent in (norm_z, meta, norm_y, words, total_y, total_z, total_era, pulls, levels):
        sent.wait_send()
    for hop in range(hops):
        for item in range(items):
            for way in range(2):
                if item in ring_items(way, hop):
                    ring_copy(way, hop, item).wait_send()
    for hop in range(stat_hops):
        for sub in range(SUBS):
            for way in range(2):
                if sub in stat_subs(way, hop):
                    stat_copy(way, hop, sub).wait_send()
    keep.wait()
    results.wait_send()
    results.wait_recv()


def body(counts, block_term, doc_year, doc_topics, log_params, drift, obs_noise):
    ne = lax.axis_size("era")
    nz = NZ
    ny = lax.axis_size("dp") // nz
    years, k, _ = log_params.shape
    rows = years * k
    nblk = counts.shape[0]
    pieces = [ring_pieces(way, ny, nz, nblk) for way in range(2)]
    sizes = (ne, ny, nz, years, k, nblk, pieces)
    bf16, f32, i32 = jnp.bfloat16, jnp.float32, jnp.int32
    hops = nz // 2
    hbm = pl.BlockSpec(memory_space=pltpu.HBM)
    operands = (
        block_term,
        doc_year,
        counts,
        doc_topics,
        log_params,
        drift.reshape(1, -1),
        obs_noise.reshape(1, -1),
    )
    landing = [
        (pltpu.SMEM if index < 2 else pltpu.VMEM)(value.shape, value.dtype) for index, value in enumerate(operands)
    ]
    slots = [pltpu.VMEM((BLOCK, k), bf16)] * nz + [pltpu.VMEM((nblk + 1, BLOCK, BLOCK), bf16)] * nz
    work = [
        pltpu.VMEM((nz, 8, BLOCK), i32),
        pltpu.SMEM((nz, 8, BLOCK), i32),
        pltpu.VMEM((rows, BLOCK), f32),
        pltpu.VMEM((years, k, ny * BLOCK), bf16),
        pltpu.VMEM((nz, 1, rows), f32),
        pltpu.VMEM((ny, 1, rows), f32),
        pltpu.VMEM((BLOCK, k), f32),
        pltpu.VMEM((rows, nz * BLOCK), bf16),
        pltpu.VMEM((nz * BLOCK, ny * BLOCK), bf16),
        pltpu.VMEM((nz, BLOCK, k), bf16),
        pltpu.VMEM((nz, BLOCK, k), bf16),
        pltpu.VMEM((2, ny // 2, rows, BLOCK), bf16),
        pltpu.VMEM((2, ny // 2, rows, BLOCK), bf16),
        pltpu.VMEM((ny, 1, rows), f32),
        pltpu.VMEM((nz, 1, rows), f32),
        pltpu.VMEM((ne, 1, rows), f32),
        pltpu.VMEM((BLOCK, k), f32),
        pltpu.VMEM((k, BLOCK), f32),
        pltpu.VMEM((ne, years, k // ne, BLOCK), bf16),
        pltpu.VMEM((ne, years, k // ne, BLOCK), bf16),
        pltpu.VMEM((ne, years, k // ne, BLOCK), bf16),
    ]
    dma = pltpu.SemaphoreType.DMA
    ring_sems = dma((2, hops, 1 + max(len(part) for part in pieces)))
    sems = [dma((len(operands),)), ring_sems, ring_sems, dma]
    for count in (nz, ny, nz, ny, nz, 0, ny, nz, ne, ne, ne):
        sems += [dma((count - 1,)) if count else dma((2, ny // 2, SUBS))] * 2
    new_topics, smoothed = pl.pallas_call(
        functools.partial(kernel, sizes),
        out_shape=(
            jax.ShapeDtypeStruct(doc_topics.shape, bf16),
            jax.ShapeDtypeStruct(log_params.shape, bf16),
        ),
        in_specs=[hbm] * len(operands),
        out_specs=(pl.BlockSpec(memory_space=pltpu.VMEM), pl.BlockSpec(memory_space=pl.ANY)),
        scratch_shapes=landing + slots + work + sems,
        compiler_params=pltpu.CompilerParams(
            collective_id=0, has_side_effects=True, vmem_limit_bytes=60 * 1024 * 1024
        ),
    )(*operands)
    return (new_topics, smoothed.astype(f32))


def solution(mesh):
    return jax.shard_map(
        body,
        mesh=mesh,
        in_specs=(
            P(("era", "dp"), None, None),
            P(("era", "dp")),
            P(("era", "dp")),
            P(("era", "dp"), None),
            P("era", None, "dp"),
            P(),
            P(),
        ),
        out_specs=(P(("era", "dp"), None), P("era", None, "dp")),
        check_vma=False,
    )
```

```python
import functools

import jax
import jax.numpy as jnp
from jax import lax
from jax.experimental import pallas as pl
from jax.experimental.pallas import tpu as pltpu
from jax.sharding import PartitionSpec as P

MESH = pl.DeviceIdType.MESH
NZ = 8
PRIOR_VARIANCE = 1.0
BLOCK = 128
SUBS = 4
LARGEST_PIECE = 4


def dot(a, b, contract):
    return lax.dot_general(a, b, (contract, ((), ())), preferred_element_type=jnp.float32)


def row_sums(value):
    return jnp.sum(jnp.transpose(value), axis=0, keepdims=True)


class Copies:
    def __init__(self, copies):
        self.copies = copies

    def start(self):
        for copy in self.copies:
            copy.start()

    def wait_recv(self):
        for copy in self.copies:
            copy.wait_recv()

    def wait_send(self):
        for copy in self.copies:
            copy.wait_send()


def remote(src, dst, send_sem, recv_sem, device):
    return pltpu.make_async_remote_copy(
        src_ref=src, dst_ref=dst, send_sem=send_sem, recv_sem=recv_sem, device_id=device, device_id_type=MESH
    )


def blocks_needed(way, hop, ny, nz, nblk):
    half = ny - ny // 2 if way else ny // 2
    return min(nblk, half + ny * (nz // 2 - 1 - hop))


def ring_pieces(way, ny, nz, nblk):
    ends = sorted({blocks_needed(way, hop, ny, nz, nblk) for hop in range(nz // 2)} | {nblk})
    parts, start = [], 0
    for end in ends:
        while start < end:
            stop = min(end, start + LARGEST_PIECE)
            parts.append((start, stop))
            start = stop
    return parts


def kernel(sizes, *refs):
    ne, ny, nz, years, k, nblk, pieces = sizes
    refs = list(refs)

    def take(count=None):
        if count is None:
            return refs.pop(0)
        return [refs.pop(0) for _ in range(count)]

    bterm_in, dyear_in, counts_in, topics_in, logp_in, drift_in, onoise_in = take(7)
    new_ref, out_ref = take(2)
    bterm, dyear, counts, topics, logp, drift, onoise = take(7)
    low = take(nz)
    cnt = take(nz)
    mbuf, msmem, expo, wbuf, nzb, nyb, scale, ptall, rall = take(9)
    pbs, pbr, sts, str_, tyb, tzb, teb, cmat, cturn, es, er, sm, land = take(13)
    in_sems, ring_send, ring_recv, local_sem = take(4)
    pairs = [take(2) for _ in range(len(refs) // 2)]
    m_sems, w_sems, nz_sems, ny_sems, pb_sems, st_sems, ty_sems, tz_sems, te_sems, es_sems, out_sems = pairs

    rows = years * k
    all_years = ne * years
    slice_rows = k // ne
    era = lax.axis_index("era")
    dp = lax.axis_index("dp")
    y = dp // nz
    z = lax.rem(dp, nz)

    def at_z(offset):
        return {"dp": y * nz + lax.rem(z + offset, nz)}

    def at_y(offset):
        return {"dp": lax.rem(y + offset, ny) * nz + z}

    def at_era(offset):
        return {"era": lax.rem(era + offset, ne)}

    def spread_out(buffer, me, count, target, sems):
        send, recv = sems
        return Copies(
            [
                remote(buffer.at[me], buffer.at[me], send.at[offset - 1], recv.at[offset - 1], target(offset))
                for offset in range(1, count)
            ]
        )

    def total_of(buffer, count):
        total = buffer[0].astype(jnp.float32)
        for slot in range(1, count):
            total = total + buffer[slot].astype(jnp.float32)
        return total

    barrier = pltpu.get_barrier_semaphore()
    for target, count in ((at_z, nz), (at_y, ny), (at_era, ne)):
        for offset in range(1, count):
            pl.semaphore_signal(barrier, inc=1, device_id=target(offset), device_id_type=MESH)
    inputs = (
        (logp_in, logp),
        (topics_in, topics),
        (counts_in, counts),
        (bterm_in, bterm),
        (dyear_in, dyear),
        (drift_in, drift),
        (onoise_in, onoise),
    )
    loads = [pltpu.make_async_copy(src, dst, in_sems.at[index]) for index, (src, dst) in enumerate(inputs)]
    for load in loads:
        load.start()

    loads[1].wait()
    proportion = topics[...].astype(jnp.float32)
    proportion = proportion / jnp.sum(proportion, axis=1, keepdims=True)
    low[0][...] = proportion.astype(jnp.bfloat16)

    norm_z = spread_out(nzb, z, nz, at_z, nz_sems)
    norm_y = spread_out(nyb, y, ny, at_y, ny_sems)
    meta = spread_out(mbuf, z, nz, at_z, m_sems)

    hops = nz // 2
    items = 1 + max(len(part) for part in pieces)

    def ring_items(way, hop):
        need = blocks_needed(way, hop, ny, nz, nblk)
        return [0] + [1 + index for index, (_, end) in enumerate(pieces[way]) if end <= need]

    def ring_copy(way, hop, item):
        here = hop if way else (nz - hop) % nz
        there = hop + 1 if way else nz - hop - 1
        if item == 0:
            src, dst = low[here], low[there]
            if hop == hops - 1:
                half = pl.ds(way * (BLOCK // 2), BLOCK // 2)
                src, dst = src.at[half], dst.at[half]
        else:
            start, end = pieces[way][item - 1]
            block = pl.ds(nblk - end if way else start, end - start)
            src, dst = cnt[here].at[block], cnt[there].at[block]
        return remote(
            src, dst, ring_send.at[way, hop, item], ring_recv.at[way, hop, item], at_z(nz - 1 if way else 1)
        )

    def ring_pass(hop, which):
        for item in which:
            for way in range(2):
                if item in ring_items(way, hop):
                    ring_copy(way, hop, item).wait_recv()
                    if hop + 1 < hops and item in ring_items(way, hop + 1):
                        ring_copy(way, hop + 1, item).start()

    pl.semaphore_wait(barrier, nz + ny + ne - 3)
    for way in range(2):
        ring_copy(way, 0, 0).start()
    loads[0].wait()
    exponent = jnp.exp(logp[...].reshape(rows, BLOCK))
    expo[...] = exponent
    nzb[z] = row_sums(exponent)
    norm_z.start()

    for load in loads[2:]:
        load.wait()
    keys, antipodal = [], 0
    for index in range(nblk):
        distance = lax.rem(lax.rem(bterm[index], nz) - z + nz, nz)
        opposite = distance == hops
        key = jnp.where(distance < hops, -distance, nz - distance)
        keys.append(jnp.where(opposite, jnp.where(antipodal < ny // 2, -hops, hops), key))
        antipodal = antipodal + jnp.where(opposite, 1, 0)
    position = [0] * nblk
    for later in range(nblk):
        for earlier in range(later):
            before = jnp.where(keys[earlier] <= keys[later], 1, 0)
            position[later] = position[later] + before
            position[earlier] = position[earlier] + (1 - before)
    length = jnp.zeros((BLOCK, BLOCK), jnp.int32)
    filled = set()
    for step in range(max(len(part) for part in pieces)):
        for way in range(2):
            if step < len(pieces[way]):
                start, end = pieces[way][step]
                if way:
                    start, end = nblk - end, nblk - start
                for place in range(start, end):
                    if place not in filled:
                        filled.add(place)
                        block = sum(jnp.where(position[index] == place, index, 0) for index in range(nblk))
                        value = counts[block]
                        length = length + value
                        cnt[0][place] = value.astype(jnp.float32).astype(jnp.bfloat16)
                if 1 + step in ring_items(way, 0):
                    ring_copy(way, 0, 1 + step).start()
    lane = lax.broadcasted_iota(jnp.int32, (8, BLOCK), 1)
    table = jnp.full((8, BLOCK), nblk, jnp.int32)
    for index in range(nblk):
        table = jnp.where(lane == bterm[index], position[index], table)
    table = jnp.where(lane == ny * nz, lax.rem(dyear[0], years), table)
    mbuf[z] = table
    meta.start()
    for slot in range(nz):
        cnt[slot][nblk] = jnp.zeros((BLOCK, BLOCK), jnp.bfloat16)
    doc_length = jnp.sum(length.astype(jnp.float32), axis=1, keepdims=True)
    scale[...] = float(k) * proportion / doc_length
    cmat[...] = jnp.zeros_like(cmat)
    cmat[all_years : all_years + 1, :] = drift[...]
    cmat[all_years + 1 : all_years + 2, :] = onoise[...]

    norm_z.wait_recv()
    nyb[y] = total_of(nzb, nz)
    norm_y.start()
    norm_y.wait_recv()
    normalizer = jnp.transpose(jnp.broadcast_to(total_of(nyb, ny), (BLOCK, rows)))
    own_columns = pl.ds(pl.multiple_of(y * BLOCK, BLOCK), BLOCK)
    wbuf[:, :, own_columns] = (expo[...] / normalizer).astype(jnp.bfloat16).reshape(years, k, BLOCK)
    own_words = wbuf.at[:, :, own_columns]
    words = Copies(
        [
            remote(own_words, own_words, w_sems[0].at[offset - 1], w_sems[1].at[offset - 1], at_y(offset))
            for offset in range(1, ny)
        ]
    )
    words.start()

    totals = [jnp.zeros((1, k), jnp.float32) for _ in range(years)]
    sub_rows = rows // SUBS
    sub_topics = k // SUBS

    def stat_rows(sub, period):
        start = sub * sub_rows + period * sub_topics
        return slice(start, start + sub_topics)

    def document_block(slot):
        source = lax.rem(z + slot, nz)
        year = msmem[source, 0, ny * nz]
        left = low[slot][...]
        table = wbuf[year]
        scores = dot(left, table, ((1,), (0,)))
        here = slice(slot * BLOCK, (slot + 1) * BLOCK)
        for column in range(ny):
            block = cnt[slot][msmem[source, 0, column * nz + z]].astype(jnp.float32)
            terms = slice(column * BLOCK, (column + 1) * BLOCK)
            rall[here, terms] = (block / scores[:, terms]).astype(jnp.bfloat16)
        pull = dot(rall[here, :], table, ((1,), (1,)))
        left = left.astype(jnp.float32)
        share = jnp.sum(left * pull, axis=0, keepdims=True)
        turned = jnp.transpose(left)
        for period in range(years):
            flag = (year == period).astype(jnp.float32)
            masked = (turned * flag).astype(jnp.bfloat16)
            for sub in range(SUBS):
                ptall[stat_rows(sub, period), here] = masked[sub * sub_topics : (sub + 1) * sub_topics]
            totals[period] = totals[period] + share * flag
        if slot == 0:
            pbr[z] = pull.astype(jnp.bfloat16)
        else:
            pbs[slot] = pull.astype(jnp.bfloat16)

    order = [0]
    for step in range(1, hops):
        order += [step, nz - step]
    order.append(hops)
    last_doc = slice(hops * BLOCK, (hops + 1) * BLOCK)

    def first_product():
        columns = pl.ds(pl.multiple_of(lax.rem(y + ny // 2, ny) * BLOCK, BLOCK), BLOCK)
        before, after = slice(0, hops * BLOCK), slice((hops + 1) * BLOCK, nz * BLOCK)
        part = dot(ptall[:, before], rall[before, columns], ((1,), (0,)))
        if nz - 1 > hops:
            part = part + dot(ptall[:, after], rall[after, columns], ((1,), (0,)))
        expo[...] = part

    early = hops > 1
    done = 0
    for hop in range(hops):
        if hop == hops - 1 and early:
            first_product()
        last = hop == hops - 2 or hops == 1
        if last:
            ring_pass(hop, range(items // 2))
            words.wait_recv()
            meta.wait_recv()
            to_smem = pltpu.make_async_copy(mbuf, msmem, local_sem)
            to_smem.start()
            to_smem.wait()
            while done < min(3, 2 * hop + 1):
                document_block(order[done])
                done += 1
            ring_pass(hop, range(items // 2, items))
        else:
            ring_pass(hop, range(0 if hop == 0 else 0, items))
        if hop >= hops - 2:
            ready = nz if hop == hops - 1 else 2 * hop + 3
            while done < ready:
                document_block(order[done])
                done += 1

    tyb[y] = jnp.concatenate(totals, axis=1)
    total_y = spread_out(tyb, y, ny, at_y, ty_sems)
    total_z = spread_out(tzb, z, nz, at_z, tz_sems)
    total_era = spread_out(teb, era, ne, at_era, te_sems)
    total_y.start()

    stat_hops = ny // 2
    jump = stat_hops > 2

    def stat_subs(way, hop):
        if hop > 0:
            return list(range(SUBS))
        return list(range(SUBS // 2)) if way == 0 else list(range(SUBS // 2, SUBS))

    def stat_copy(way, hop, sub):
        part = pl.ds(sub * sub_rows, sub_rows)
        steps = 2 if jump and hop == 0 else 1
        return remote(
            sts.at[way, hop, part],
            str_.at[way, hop, part],
            st_sems[0].at[way, hop, sub],
            st_sems[1].at[way, hop, sub],
            at_y(ny - steps if way else steps),
        )

    def came_from(hop):
        if jump:
            return [[], [], [0, 1]][hop] if hop < 3 else [hop - 1]
        return [hop - 1] if hop else []

    def stat_block(offset):
        columns = pl.ds(pl.multiple_of(lax.rem(y + offset, ny) * BLOCK, BLOCK), BLOCK)
        if early and offset == stat_hops:
            part = expo[...] + dot(ptall[:, last_doc], rall[last_doc, columns], ((1,), (0,)))
        else:
            part = dot(ptall[...], rall[:, columns], ((1,), (0,)))
        words_here = [
            wbuf[period, sub * sub_topics : (sub + 1) * sub_topics, columns]
            for sub in range(SUBS)
            for period in range(years)
        ]
        return part * jnp.concatenate(words_here, axis=0).astype(jnp.float32)

    terms = float(ny * nz * BLOCK)
    pulls = Copies(
        [
            remote(pbs.at[offset], pbr.at[z], pb_sems[0].at[offset - 1], pb_sems[1].at[offset - 1], at_z(offset))
            for offset in range(1, nz)
        ]
    )

    def after_y():
        total_y.wait_recv()
        tzb[z] = total_of(tyb, ny)
        total_z.start()

    def after_z():
        total_z.wait_recv()
        teb[era] = jnp.log(terms) - jnp.log(total_of(tzb, nz) + terms)
        total_era.start()
        pulls.start()

    def after_era():
        total_era.wait_recv()
        for index in range(ne):
            for period in range(years):
                line = index * years + period
                cmat[line : line + 1, :] = teb[index, :, period * k : (period + 1) * k]
        cturn[...] = jnp.transpose(cmat[...])

    beside = [after_y, after_z, after_era]
    for hop in range(stat_hops):
        distance = stat_hops - hop
        parts = [stat_block(distance)]
        parts.append(parts[0] if hop == 0 else stat_block(ny - distance))
        if hop > int(jump) and beside:
            beside.pop(0)()
        for sub in range(SUBS):
            part = slice(sub * sub_rows, (sub + 1) * sub_rows)
            for way in range(2):
                if sub in stat_subs(way, hop):
                    value = parts[way][part]
                    for source in came_from(hop):
                        if sub in stat_subs(way, source):
                            stat_copy(way, source, sub).wait_recv()
                            value = value + str_[way, source, part, :].astype(jnp.float32)
                    sts[way, hop, part, :] = value.astype(jnp.bfloat16)
                    stat_copy(way, hop, sub).start()
    own_part = stat_block(0)
    for step in beside:
        step()

    def slice_of(offset):
        return pl.ds(pl.multiple_of(lax.rem(era + offset, ne) * slice_rows, slice_rows), slice_rows)

    own_slice = slice_of(0)

    def level_copy(peer):
        return remote(es.at[peer], er.at[era], es_sems[0].at[peer], es_sems[1].at[era], {"era": peer})

    sent = 0
    for sub in range(SUBS):
        part = slice(sub * sub_rows, (sub + 1) * sub_rows)
        value = own_part[part]
        for way in range(2):
            if sub in stat_subs(way, stat_hops - 1):
                stat_copy(way, stat_hops - 1, sub).wait_recv()
                value = value + str_[way, stat_hops - 1, part, :].astype(jnp.float32)
        value = value.astype(jnp.bfloat16)
        step = min(slice_rows, sub_topics)
        for period in range(years):
            for start in range(0, sub_topics, step):
                topic = sub * sub_topics + start
                rows_here = slice(topic % slice_rows, topic % slice_rows + step)
                es[topic // slice_rows, period, rows_here, :] = value[
                    period * sub_topics + start : period * sub_topics + start + step
                ]
        while (sent + 1) * slice_rows <= (sub + 1) * sub_topics:
            pl.when(era != sent)(level_copy(sent).start)
            sent += 1
    er[era] = es[era]
    columns = cturn[own_slice, :]

    def column(index):
        return jnp.broadcast_to(columns[:, index : index + 1], (slice_rows, BLOCK))

    spread = column(all_years)
    noise_scale = column(all_years + 1)
    for offset in range(1, ne):
        sender = lax.rem(era + offset, ne)
        remote(es.at[sender], er.at[sender], es_sems[0].at[sender], es_sems[1].at[sender], at_era(offset)).wait_recv()

    variance = jnp.full((slice_rows, BLOCK), PRIOR_VARIANCE, jnp.float32)
    mean = jnp.zeros((slice_rows, BLOCK), jnp.float32)
    means, weights = [], []
    for period in range(all_years):
        level = jnp.log(er[period // years, period % years].astype(jnp.float32) + 1.0)
        observed = level + column(period)
        noise = noise_scale / (1.0 + level)
        predicted = variance + spread
        gain = predicted / (predicted + noise)
        mean = mean + gain * (observed - mean)
        variance = gain * noise
        means.append(mean)
        weights.append(variance / (variance + spread))
    smooth = means[-1]
    sm[ne - 1, years - 1] = smooth.astype(sm.dtype)
    for period in range(all_years - 2, -1, -1):
        smooth = means[period] + weights[period] * (smooth - means[period])
        sm[period // years, period % years] = smooth.astype(sm.dtype)

    land[era] = sm[era]
    results = Copies(
        [
            remote(
                sm.at[lax.rem(era + offset, ne)],
                land.at[era],
                out_sems[0].at[offset - 1],
                out_sems[1].at[offset - 1],
                at_era(offset),
            )
            for offset in range(1, ne)
        ]
    )
    results.start()
    pulls.wait_recv()
    new_ref[...] = (scale[...] * total_of(pbr, nz)).astype(jnp.bfloat16)
    for sent in (norm_z, meta, norm_y, words, total_y, total_z, total_era, pulls):
        sent.wait_send()
    for hop in range(hops):
        for item in range(items):
            for way in range(2):
                if item in ring_items(way, hop):
                    ring_copy(way, hop, item).wait_send()
    for hop in range(stat_hops):
        for sub in range(SUBS):
            for way in range(2):
                if sub in stat_subs(way, hop):
                    stat_copy(way, hop, sub).wait_send()
    for offset in range(1, ne):
        level_copy(lax.rem(era + offset, ne)).wait_send()
    results.wait_recv()
    for index in range(ne):
        out_ref[:, index * slice_rows : (index + 1) * slice_rows, :] = land[index].astype(out_ref.dtype)
    results.wait_send()


def body(counts, block_term, doc_year, doc_topics, log_params, drift, obs_noise):
    ne = lax.axis_size("era")
    nz = NZ
    ny = lax.axis_size("dp") // nz
    years, k, _ = log_params.shape
    rows = years * k
    nblk = counts.shape[0]
    pieces = [ring_pieces(way, ny, nz, nblk) for way in range(2)]
    sizes = (ne, ny, nz, years, k, nblk, pieces)
    bf16, f32, i32 = jnp.bfloat16, jnp.float32, jnp.int32
    hops = nz // 2
    hbm = pl.BlockSpec(memory_space=pltpu.HBM)
    operands = (
        block_term,
        doc_year,
        counts,
        doc_topics,
        log_params,
        drift.reshape(1, -1),
        obs_noise.reshape(1, -1),
    )
    landing = [
        (pltpu.SMEM if index < 2 else pltpu.VMEM)(value.shape, value.dtype) for index, value in enumerate(operands)
    ]
    slots = [pltpu.VMEM((BLOCK, k), bf16)] * nz + [pltpu.VMEM((nblk + 1, BLOCK, BLOCK), bf16)] * nz
    work = [
        pltpu.VMEM((nz, 8, BLOCK), i32),
        pltpu.SMEM((nz, 8, BLOCK), i32),
        pltpu.VMEM((rows, BLOCK), f32),
        pltpu.VMEM((years, k, ny * BLOCK), bf16),
        pltpu.VMEM((nz, 1, rows), f32),
        pltpu.VMEM((ny, 1, rows), f32),
        pltpu.VMEM((BLOCK, k), f32),
        pltpu.VMEM((rows, nz * BLOCK), bf16),
        pltpu.VMEM((nz * BLOCK, ny * BLOCK), bf16),
        pltpu.VMEM((nz, BLOCK, k), bf16),
        pltpu.VMEM((nz, BLOCK, k), bf16),
        pltpu.VMEM((2, ny // 2, rows, BLOCK), bf16),
        pltpu.VMEM((2, ny // 2, rows, BLOCK), bf16),
        pltpu.VMEM((ny, 1, rows), f32),
        pltpu.VMEM((nz, 1, rows), f32),
        pltpu.VMEM((ne, 1, rows), f32),
        pltpu.VMEM((BLOCK, k), f32),
        pltpu.VMEM((k, BLOCK), f32),
        pltpu.VMEM((ne, years, k // ne, BLOCK), bf16),
        pltpu.VMEM((ne, years, k // ne, BLOCK), bf16),
        pltpu.VMEM((ne, years, k // ne, BLOCK), bf16),
        pltpu.VMEM((ne, years, k // ne, BLOCK), bf16),
    ]
    dma = pltpu.SemaphoreType.DMA
    ring_sems = dma((2, hops, 1 + max(len(part) for part in pieces)))
    sems = [dma((len(operands),)), ring_sems, ring_sems, dma]
    for count in (nz, ny, nz, ny, nz, 0, ny, nz, ne, ne + 1, ne):
        sems += [dma((count - 1,)) if count else dma((2, ny // 2, SUBS))] * 2
    new_topics, smoothed = pl.pallas_call(
        functools.partial(kernel, sizes),
        out_shape=(
            jax.ShapeDtypeStruct(doc_topics.shape, bf16),
            jax.ShapeDtypeStruct(log_params.shape, bf16),
        ),
        in_specs=[hbm] * len(operands),
        out_specs=(pl.BlockSpec(memory_space=pltpu.VMEM), pl.BlockSpec(memory_space=pltpu.VMEM)),
        scratch_shapes=landing + slots + work + sems,
        compiler_params=pltpu.CompilerParams(
            collective_id=0, has_side_effects=True, vmem_limit_bytes=60 * 1024 * 1024
        ),
    )(*operands)
    return (new_topics, smoothed.astype(f32))


def solution(mesh):
    return jax.shard_map(
        body,
        mesh=mesh,
        in_specs=(
            P(("era", "dp"), None, None),
            P(("era", "dp")),
            P(("era", "dp")),
            P(("era", "dp"), None),
            P("era", None, "dp"),
            P(),
            P(),
        ),
        out_specs=(P(("era", "dp"), None), P("era", None, "dp")),
        check_vma=False,
    )
```

```python
import functools

import jax
import jax.numpy as jnp
from jax import lax
from jax.experimental import pallas as pl
from jax.experimental.pallas import tpu as pltpu
from jax.sharding import PartitionSpec as P

MESH = pl.DeviceIdType.MESH
NZ = 8
PRIOR_VARIANCE = 1.0
BLOCK = 128
SUBS = 4
LARGEST_PIECE = 8


def dot(a, b, contract):
    return lax.dot_general(a, b, (contract, ((), ())), preferred_element_type=jnp.float32)


def row_sums(value):
    return jnp.sum(jnp.transpose(value), axis=0, keepdims=True)


class Copies:
    def __init__(self, copies):
        self.copies = copies

    def start(self):
        for copy in self.copies:
            copy.start()

    def wait_recv(self):
        for copy in self.copies:
            copy.wait_recv()

    def wait_send(self):
        for copy in self.copies:
            copy.wait_send()


def remote(src, dst, send_sem, recv_sem, device):
    return pltpu.make_async_remote_copy(
        src_ref=src, dst_ref=dst, send_sem=send_sem, recv_sem=recv_sem, device_id=device, device_id_type=MESH
    )


def blocks_needed(way, hop, ny, nz, nblk):
    half = ny - ny // 2 if way else ny // 2
    return min(nblk, half + ny * (nz // 2 - 1 - hop))


def ring_pieces(way, ny, nz, nblk):
    ends = sorted({blocks_needed(way, hop, ny, nz, nblk) for hop in range(nz // 2)} | {nblk})
    parts, start = [], 0
    for end in ends:
        while start < end:
            stop = min(end, start + LARGEST_PIECE)
            parts.append((start, stop))
            start = stop
    return parts


def kernel(sizes, *refs):
    ne, ny, nz, years, k, nblk, pieces = sizes
    refs = list(refs)

    def take(count=None):
        if count is None:
            return refs.pop(0)
        return [refs.pop(0) for _ in range(count)]

    bterm_in, dyear_in, counts_in, topics_in, logp_in, drift_in, onoise_in = take(7)
    new_ref, out_ref = take(2)
    bterm, dyear, counts, topics, logp, drift, onoise = take(7)
    low = take(nz)
    cnt = take(nz)
    mbuf, msmem, expo, wbuf, nzb, nyb, scale, ptall, rall = take(9)
    pbs, pbr, sts, str_, tyb, tzb, teb, cmat, cturn, es, er, sm, land = take(13)
    in_sems, ring_send, ring_recv, local_sem = take(4)
    pairs = [take(2) for _ in range(len(refs) // 2)]
    m_sems, w_sems, nz_sems, ny_sems, pb_sems, st_sems, ty_sems, tz_sems, te_sems, es_sems, out_sems = pairs

    rows = years * k
    all_years = ne * years
    slice_rows = k // ne
    era = lax.axis_index("era")
    dp = lax.axis_index("dp")
    y = dp // nz
    z = lax.rem(dp, nz)

    def at_z(offset):
        return {"dp": y * nz + lax.rem(z + offset, nz)}

    def at_y(offset):
        return {"dp": lax.rem(y + offset, ny) * nz + z}

    def at_era(offset):
        return {"era": lax.rem(era + offset, ne)}

    def spread_out(buffer, me, count, target, sems):
        send, recv = sems
        return Copies(
            [
                remote(buffer.at[me], buffer.at[me], send.at[offset - 1], recv.at[offset - 1], target(offset))
                for offset in range(1, count)
            ]
        )

    def total_of(buffer, count):
        total = buffer[0].astype(jnp.float32)
        for slot in range(1, count):
            total = total + buffer[slot].astype(jnp.float32)
        return total

    barrier = pltpu.get_barrier_semaphore()
    for target, count in ((at_z, nz), (at_y, ny), (at_era, ne)):
        for offset in range(1, count):
            pl.semaphore_signal(barrier, inc=1, device_id=target(offset), device_id_type=MESH)
    inputs = (
        (logp_in, logp),
        (topics_in, topics),
        (counts_in, counts),
        (bterm_in, bterm),
        (dyear_in, dyear),
        (drift_in, drift),
        (onoise_in, onoise),
    )
    loads = [pltpu.make_async_copy(src, dst, in_sems.at[index]) for index, (src, dst) in enumerate(inputs)]
    for load in loads:
        load.start()

    loads[1].wait()
    proportion = topics[...].astype(jnp.float32)
    proportion = proportion / jnp.sum(proportion, axis=1, keepdims=True)
    low[0][...] = proportion.astype(jnp.bfloat16)

    norm_z = spread_out(nzb, z, nz, at_z, nz_sems)
    norm_y = spread_out(nyb, y, ny, at_y, ny_sems)
    meta = spread_out(mbuf, z, nz, at_z, m_sems)

    hops = nz // 2
    items = 1 + max(len(part) for part in pieces)

    def ring_items(way, hop):
        need = blocks_needed(way, hop, ny, nz, nblk)
        return [0] + [1 + index for index, (_, end) in enumerate(pieces[way]) if end <= need]

    def ring_copy(way, hop, item):
        here = hop if way else (nz - hop) % nz
        there = hop + 1 if way else nz - hop - 1
        if item == 0:
            src, dst = low[here], low[there]
            if hop == hops - 1:
                half = pl.ds(way * (BLOCK // 2), BLOCK // 2)
                src, dst = src.at[half], dst.at[half]
        else:
            start, end = pieces[way][item - 1]
            block = pl.ds(nblk - end if way else start, end - start)
            src, dst = cnt[here].at[block], cnt[there].at[block]
        return remote(
            src, dst, ring_send.at[way, hop, item], ring_recv.at[way, hop, item], at_z(nz - 1 if way else 1)
        )

    def ring_pass(hop, which):
        for item in which:
            for way in range(2):
                if item in ring_items(way, hop):
                    ring_copy(way, hop, item).wait_recv()
                    if hop + 1 < hops and item in ring_items(way, hop + 1):
                        ring_copy(way, hop + 1, item).start()

    pl.semaphore_wait(barrier, nz + ny + ne - 3)
    for way in range(2):
        ring_copy(way, 0, 0).start()
    loads[0].wait()
    exponent = jnp.exp(logp[...].reshape(rows, BLOCK))
    expo[...] = exponent
    nzb[z] = row_sums(exponent)
    norm_z.start()

    for load in loads[2:]:
        load.wait()
    keys, antipodal = [], 0
    for index in range(nblk):
        distance = lax.rem(lax.rem(bterm[index], nz) - z + nz, nz)
        opposite = distance == hops
        key = jnp.where(distance < hops, -distance, nz - distance)
        keys.append(jnp.where(opposite, jnp.where(antipodal < ny // 2, -hops, hops), key))
        antipodal = antipodal + jnp.where(opposite, 1, 0)
    position = [0] * nblk
    for later in range(nblk):
        for earlier in range(later):
            before = jnp.where(keys[earlier] <= keys[later], 1, 0)
            position[later] = position[later] + before
            position[earlier] = position[earlier] + (1 - before)
    length = jnp.zeros((BLOCK, BLOCK), jnp.int32)
    filled = set()
    for step in range(max(len(part) for part in pieces)):
        for way in range(2):
            if step < len(pieces[way]):
                start, end = pieces[way][step]
                if way:
                    start, end = nblk - end, nblk - start
                for place in range(start, end):
                    if place not in filled:
                        filled.add(place)
                        block = sum(jnp.where(position[index] == place, index, 0) for index in range(nblk))
                        value = counts[block]
                        length = length + value
                        cnt[0][place] = value.astype(jnp.float32).astype(jnp.bfloat16)
                if 1 + step in ring_items(way, 0):
                    ring_copy(way, 0, 1 + step).start()
    lane = lax.broadcasted_iota(jnp.int32, (8, BLOCK), 1)
    table = jnp.full((8, BLOCK), nblk, jnp.int32)
    for index in range(nblk):
        table = jnp.where(lane == bterm[index], position[index], table)
    table = jnp.where(lane == ny * nz, lax.rem(dyear[0], years), table)
    mbuf[z] = table
    meta.start()
    for slot in range(nz):
        cnt[slot][nblk] = jnp.zeros((BLOCK, BLOCK), jnp.bfloat16)
    doc_length = jnp.sum(length.astype(jnp.float32), axis=1, keepdims=True)
    scale[...] = float(k) * proportion / doc_length
    cmat[...] = jnp.zeros_like(cmat)
    cmat[all_years : all_years + 1, :] = drift[...]
    cmat[all_years + 1 : all_years + 2, :] = onoise[...]

    norm_z.wait_recv()
    nyb[y] = total_of(nzb, nz)
    norm_y.start()
    norm_y.wait_recv()
    normalizer = jnp.transpose(jnp.broadcast_to(total_of(nyb, ny), (BLOCK, rows)))
    own_columns = pl.ds(pl.multiple_of(y * BLOCK, BLOCK), BLOCK)
    wbuf[:, :, own_columns] = (expo[...] / normalizer).astype(jnp.bfloat16).reshape(years, k, BLOCK)
    own_words = wbuf.at[:, :, own_columns]
    words = Copies(
        [
            remote(own_words, own_words, w_sems[0].at[offset - 1], w_sems[1].at[offset - 1], at_y(offset))
            for offset in range(1, ny)
        ]
    )
    words.start()

    totals = [jnp.zeros((1, k), jnp.float32) for _ in range(years)]
    sub_rows = rows // SUBS
    sub_topics = k // SUBS

    def stat_rows(sub, period):
        start = sub * sub_rows + period * sub_topics
        return slice(start, start + sub_topics)

    def document_block(slot):
        source = lax.rem(z + slot, nz)
        year = msmem[source, 0, ny * nz]
        left = low[slot][...]
        table = wbuf[year]
        scores = dot(left, table, ((1,), (0,)))
        here = slice(slot * BLOCK, (slot + 1) * BLOCK)
        for column in range(ny):
            block = cnt[slot][msmem[source, 0, column * nz + z]].astype(jnp.float32)
            terms = slice(column * BLOCK, (column + 1) * BLOCK)
            rall[here, terms] = (block / scores[:, terms]).astype(jnp.bfloat16)
        pull = dot(rall[here, :], table, ((1,), (1,)))
        left = left.astype(jnp.float32)
        share = jnp.sum(left * pull, axis=0, keepdims=True)
        turned = jnp.transpose(left)
        for period in range(years):
            flag = (year == period).astype(jnp.float32)
            masked = (turned * flag).astype(jnp.bfloat16)
            for sub in range(SUBS):
                ptall[stat_rows(sub, period), here] = masked[sub * sub_topics : (sub + 1) * sub_topics]
            totals[period] = totals[period] + share * flag
        if slot == 0:
            pbr[z] = pull.astype(jnp.bfloat16)
        else:
            pbs[slot] = pull.astype(jnp.bfloat16)

    order = [0]
    for step in range(1, hops):
        order += [step, nz - step]
    order.append(hops)
    last_doc = slice(hops * BLOCK, (hops + 1) * BLOCK)

    def first_product():
        columns = pl.ds(pl.multiple_of(lax.rem(y + ny // 2, ny) * BLOCK, BLOCK), BLOCK)
        before, after = slice(0, hops * BLOCK), slice((hops + 1) * BLOCK, nz * BLOCK)
        part = dot(ptall[:, before], rall[before, columns], ((1,), (0,)))
        if nz - 1 > hops:
            part = part + dot(ptall[:, after], rall[after, columns], ((1,), (0,)))
        expo[...] = part

    early = hops > 1
    done = 0
    for hop in range(hops):
        if hop == hops - 1 and early:
            first_product()
        last = hop == hops - 2 or hops == 1
        if last:
            ring_pass(hop, range(items // 2))
            words.wait_recv()
            meta.wait_recv()
            to_smem = pltpu.make_async_copy(mbuf, msmem, local_sem)
            to_smem.start()
            to_smem.wait()
            while done < min(3, 2 * hop + 1):
                document_block(order[done])
                done += 1
            ring_pass(hop, range(items // 2, items))
        else:
            ring_pass(hop, range(0 if hop == 0 else 0, items))
        if hop >= hops - 2:
            ready = nz if hop == hops - 1 else 2 * hop + 3
            while done < ready:
                document_block(order[done])
                done += 1

    tyb[y] = jnp.concatenate(totals, axis=1)
    total_y = spread_out(tyb, y, ny, at_y, ty_sems)
    total_z = spread_out(tzb, z, nz, at_z, tz_sems)
    total_era = spread_out(teb, era, ne, at_era, te_sems)
    total_y.start()

    stat_hops = ny // 2
    jump = stat_hops > 2

    def stat_subs(way, hop):
        if hop > 0:
            return list(range(SUBS))
        return list(range(SUBS // 2)) if way == 0 else list(range(SUBS // 2, SUBS))

    def stat_copy(way, hop, sub):
        part = pl.ds(sub * sub_rows, sub_rows)
        steps = 2 if jump and hop == 0 else 1
        return remote(
            sts.at[way, hop, part],
            str_.at[way, hop, part],
            st_sems[0].at[way, hop, sub],
            st_sems[1].at[way, hop, sub],
            at_y(ny - steps if way else steps),
        )

    def came_from(hop):
        if jump:
            return [[], [], [0, 1]][hop] if hop < 3 else [hop - 1]
        return [hop - 1] if hop else []

    def stat_block(offset):
        columns = pl.ds(pl.multiple_of(lax.rem(y + offset, ny) * BLOCK, BLOCK), BLOCK)
        if early and offset == stat_hops:
            part = expo[...] + dot(ptall[:, last_doc], rall[last_doc, columns], ((1,), (0,)))
        else:
            part = dot(ptall[...], rall[:, columns], ((1,), (0,)))
        words_here = [
            wbuf[period, sub * sub_topics : (sub + 1) * sub_topics, columns]
            for sub in range(SUBS)
            for period in range(years)
        ]
        return part * jnp.concatenate(words_here, axis=0).astype(jnp.float32)

    terms = float(ny * nz * BLOCK)
    pulls = Copies(
        [
            remote(pbs.at[offset], pbr.at[z], pb_sems[0].at[offset - 1], pb_sems[1].at[offset - 1], at_z(offset))
            for offset in range(1, nz)
        ]
    )

    def after_y():
        total_y.wait_recv()
        tzb[z] = total_of(tyb, ny)
        total_z.start()
        pulls.start()

    def after_z():
        total_z.wait_recv()
        teb[era] = jnp.log(terms) - jnp.log(total_of(tzb, nz) + terms)
        total_era.start()

    def after_era():
        total_era.wait_recv()
        for index in range(ne):
            for period in range(years):
                line = index * years + period
                cmat[line : line + 1, :] = teb[index, :, period * k : (period + 1) * k]
        cturn[...] = jnp.transpose(cmat[...])

    beside = [after_y, after_z, after_era]
    for hop in range(stat_hops):
        distance = stat_hops - hop
        parts = [stat_block(distance)]
        parts.append(parts[0] if hop == 0 else stat_block(ny - distance))
        for sub in range(SUBS):
            part = slice(sub * sub_rows, (sub + 1) * sub_rows)
            for way in range(2):
                if sub in stat_subs(way, hop):
                    value = parts[way][part]
                    for source in came_from(hop):
                        if sub in stat_subs(way, source):
                            stat_copy(way, source, sub).wait_recv()
                            value = value + str_[way, source, part, :].astype(jnp.float32)
                    sts[way, hop, part, :] = value.astype(jnp.bfloat16)
                    stat_copy(way, hop, sub).start()
        if hop > int(jump) and len(beside) > 1:
            beside.pop(0)()
    own_part = stat_block(0)
    while len(beside) > 1:
        beside.pop(0)()

    def slice_of(offset):
        return pl.ds(pl.multiple_of(lax.rem(era + offset, ne) * slice_rows, slice_rows), slice_rows)

    own_slice = slice_of(0)

    def level_copy(peer):
        return remote(es.at[peer], er.at[era], es_sems[0].at[peer], es_sems[1].at[era], {"era": peer})

    sent = 0
    for sub in range(SUBS):
        part = slice(sub * sub_rows, (sub + 1) * sub_rows)
        value = own_part[part]
        for way in range(2):
            if sub in stat_subs(way, stat_hops - 1):
                stat_copy(way, stat_hops - 1, sub).wait_recv()
                value = value + str_[way, stat_hops - 1, part, :].astype(jnp.float32)
        value = value.astype(jnp.bfloat16)
        step = min(slice_rows, sub_topics)
        for period in range(years):
            for start in range(0, sub_topics, step):
                topic = sub * sub_topics + start
                rows_here = slice(topic % slice_rows, topic % slice_rows + step)
                es[topic // slice_rows, period, rows_here, :] = value[
                    period * sub_topics + start : period * sub_topics + start + step
                ]
        while (sent + 1) * slice_rows <= (sub + 1) * sub_topics:
            pl.when(era != sent)(level_copy(sent).start)
            sent += 1
    er[era] = es[era]
    beside.pop(0)()
    columns = cturn[own_slice, :]

    def column(index):
        return jnp.broadcast_to(columns[:, index : index + 1], (slice_rows, BLOCK))

    spread = column(all_years)
    noise_scale = column(all_years + 1)
    for offset in range(1, ne):
        sender = lax.rem(era + offset, ne)
        remote(es.at[sender], er.at[sender], es_sems[0].at[sender], es_sems[1].at[sender], at_era(offset)).wait_recv()

    variance = jnp.full((slice_rows, BLOCK), PRIOR_VARIANCE, jnp.float32)
    mean = jnp.zeros((slice_rows, BLOCK), jnp.float32)
    means, weights = [], []
    for period in range(all_years):
        level = jnp.log(er[period // years, period % years].astype(jnp.float32) + 1.0)
        observed = level + column(period)
        noise = noise_scale / (1.0 + level)
        predicted = variance + spread
        gain = predicted / (predicted + noise)
        mean = mean + gain * (observed - mean)
        variance = gain * noise
        means.append(mean)
        weights.append(variance / (variance + spread))
    smooth = means[-1]
    sm[ne - 1, years - 1] = smooth.astype(sm.dtype)
    for period in range(all_years - 2, -1, -1):
        smooth = means[period] + weights[period] * (smooth - means[period])
        sm[period // years, period % years] = smooth.astype(sm.dtype)

    land[era] = sm[era]
    results = Copies(
        [
            remote(
                sm.at[lax.rem(era + offset, ne)],
                land.at[era],
                out_sems[0].at[offset - 1],
                out_sems[1].at[offset - 1],
                at_era(offset),
            )
            for offset in range(1, ne)
        ]
    )
    results.start()
    pulls.wait_recv()
    new_ref[...] = (scale[...] * total_of(pbr, nz)).astype(jnp.bfloat16)
    for sent in (norm_z, meta, norm_y, words, total_y, total_z, total_era, pulls):
        sent.wait_send()
    for hop in range(hops):
        for item in range(items):
            for way in range(2):
                if item in ring_items(way, hop):
                    ring_copy(way, hop, item).wait_send()
    for hop in range(stat_hops):
        for sub in range(SUBS):
            for way in range(2):
                if sub in stat_subs(way, hop):
                    stat_copy(way, hop, sub).wait_send()
    for offset in range(1, ne):
        level_copy(lax.rem(era + offset, ne)).wait_send()
    results.wait_recv()
    for index in range(ne):
        out_ref[:, index * slice_rows : (index + 1) * slice_rows, :] = land[index].astype(out_ref.dtype)
    results.wait_send()


def body(counts, block_term, doc_year, doc_topics, log_params, drift, obs_noise):
    ne = lax.axis_size("era")
    nz = NZ
    ny = lax.axis_size("dp") // nz
    years, k, _ = log_params.shape
    rows = years * k
    nblk = counts.shape[0]
    pieces = [ring_pieces(way, ny, nz, nblk) for way in range(2)]
    sizes = (ne, ny, nz, years, k, nblk, pieces)
    bf16, f32, i32 = jnp.bfloat16, jnp.float32, jnp.int32
    hops = nz // 2
    hbm = pl.BlockSpec(memory_space=pltpu.HBM)
    operands = (
        block_term,
        doc_year,
        counts,
        doc_topics,
        log_params,
        drift.reshape(1, -1),
        obs_noise.reshape(1, -1),
    )
    landing = [
        (pltpu.SMEM if index < 2 else pltpu.VMEM)(value.shape, value.dtype) for index, value in enumerate(operands)
    ]
    slots = [pltpu.VMEM((BLOCK, k), bf16)] * nz + [pltpu.VMEM((nblk + 1, BLOCK, BLOCK), bf16)] * nz
    work = [
        pltpu.VMEM((nz, 8, BLOCK), i32),
        pltpu.SMEM((nz, 8, BLOCK), i32),
        pltpu.VMEM((rows, BLOCK), f32),
        pltpu.VMEM((years, k, ny * BLOCK), bf16),
        pltpu.VMEM((nz, 1, rows), f32),
        pltpu.VMEM((ny, 1, rows), f32),
        pltpu.VMEM((BLOCK, k), f32),
        pltpu.VMEM((rows, nz * BLOCK), bf16),
        pltpu.VMEM((nz * BLOCK, ny * BLOCK), bf16),
        pltpu.VMEM((nz, BLOCK, k), bf16),
        pltpu.VMEM((nz, BLOCK, k), bf16),
        pltpu.VMEM((2, ny // 2, rows, BLOCK), bf16),
        pltpu.VMEM((2, ny // 2, rows, BLOCK), bf16),
        pltpu.VMEM((ny, 1, rows), f32),
        pltpu.VMEM((nz, 1, rows), f32),
        pltpu.VMEM((ne, 1, rows), f32),
        pltpu.VMEM((BLOCK, k), f32),
        pltpu.VMEM((k, BLOCK), f32),
        pltpu.VMEM((ne, years, k // ne, BLOCK), bf16),
        pltpu.VMEM((ne, years, k // ne, BLOCK), bf16),
        pltpu.VMEM((ne, years, k // ne, BLOCK), bf16),
        pltpu.VMEM((ne, years, k // ne, BLOCK), bf16),
    ]
    dma = pltpu.SemaphoreType.DMA
    ring_sems = dma((2, hops, 1 + max(len(part) for part in pieces)))
    sems = [dma((len(operands),)), ring_sems, ring_sems, dma]
    for count in (nz, ny, nz, ny, nz, 0, ny, nz, ne, ne + 1, ne):
        sems += [dma((count - 1,)) if count else dma((2, ny // 2, SUBS))] * 2
    new_topics, smoothed = pl.pallas_call(
        functools.partial(kernel, sizes),
        out_shape=(
            jax.ShapeDtypeStruct(doc_topics.shape, bf16),
            jax.ShapeDtypeStruct(log_params.shape, bf16),
        ),
        in_specs=[hbm] * len(operands),
        out_specs=(pl.BlockSpec(memory_space=pltpu.VMEM), pl.BlockSpec(memory_space=pltpu.VMEM)),
        scratch_shapes=landing + slots + work + sems,
        compiler_params=pltpu.CompilerParams(
            collective_id=0, has_side_effects=True, vmem_limit_bytes=60 * 1024 * 1024
        ),
    )(*operands)
    return (new_topics, smoothed.astype(f32))


def solution(mesh):
    return jax.shard_map(
        body,
        mesh=mesh,
        in_specs=(
            P(("era", "dp"), None, None),
            P(("era", "dp")),
            P(("era", "dp")),
            P(("era", "dp"), None),
            P("era", None, "dp"),
            P(),
            P(),
        ),
        out_specs=(P(("era", "dp"), None), P("era", None, "dp")),
        check_vma=False,
    )
```

```python
import functools

import jax
import jax.numpy as jnp
from jax import lax
from jax.experimental import pallas as pl
from jax.experimental.pallas import tpu as pltpu
from jax.sharding import PartitionSpec as P

MESH = pl.DeviceIdType.MESH
NZ = 8
PRIOR_VARIANCE = 1.0
BLOCK = 128
SUBS = 4
LARGEST_PIECE = 8


def dot(a, b, contract):
    return lax.dot_general(a, b, (contract, ((), ())), preferred_element_type=jnp.float32)


def row_sums(value):
    return jnp.sum(jnp.transpose(value), axis=0, keepdims=True)


class Copies:
    def __init__(self, copies):
        self.copies = copies

    def start(self):
        for copy in self.copies:
            copy.start()

    def wait_recv(self):
        for copy in self.copies:
            copy.wait_recv()

    def wait_send(self):
        for copy in self.copies:
            copy.wait_send()


def remote(src, dst, send_sem, recv_sem, device):
    return pltpu.make_async_remote_copy(
        src_ref=src, dst_ref=dst, send_sem=send_sem, recv_sem=recv_sem, device_id=device, device_id_type=MESH
    )


def blocks_needed(way, hop, ny, nz, nblk):
    half = ny - ny // 2 if way else ny // 2
    return min(nblk, half + ny * (nz // 2 - 1 - hop))


def ring_pieces(way, ny, nz, nblk):
    ends = sorted({blocks_needed(way, hop, ny, nz, nblk) for hop in range(nz // 2)} | {nblk})
    parts, start = [], 0
    for end in ends:
        while start < end:
            stop = min(end, start + LARGEST_PIECE)
            parts.append((start, stop))
            start = stop
    return parts


def kernel(sizes, *refs):
    ne, ny, nz, years, k, nblk, pieces = sizes
    refs = list(refs)

    def take(count=None):
        if count is None:
            return refs.pop(0)
        return [refs.pop(0) for _ in range(count)]

    bterm_in, dyear_in, counts_in, topics_in, logp_in, drift_in, onoise_in = take(7)
    new_ref, out_ref = take(2)
    bterm, dyear, counts, topics, logp, drift, onoise = take(7)
    low = take(nz)
    cnt = take(nz)
    mbuf, msmem, expo, wbuf, nzb, nyb, scale, ptall, rall = take(9)
    pbs, pbr, sts, str_, tyb, tzb, teb, cmat, cturn, es, er, sm, land = take(13)
    in_sems, ring_send, ring_recv, local_sem = take(4)
    pairs = [take(2) for _ in range(len(refs) // 2)]
    m_sems, w_sems, nz_sems, ny_sems, pb_sems, st_sems, ty_sems, tz_sems, te_sems, es_sems, out_sems = pairs

    rows = years * k
    all_years = ne * years
    slice_rows = k // ne
    era = lax.axis_index("era")
    dp = lax.axis_index("dp")
    y = dp // nz
    z = lax.rem(dp, nz)

    def at_z(offset):
        return {"dp": y * nz + lax.rem(z + offset, nz)}

    def at_y(offset):
        return {"dp": lax.rem(y + offset, ny) * nz + z}

    def at_era(offset):
        return {"era": lax.rem(era + offset, ne)}

    def spread_out(buffer, me, count, target, sems):
        send, recv = sems
        return Copies(
            [
                remote(buffer.at[me], buffer.at[me], send.at[offset - 1], recv.at[offset - 1], target(offset))
                for offset in range(1, count)
            ]
        )

    def total_of(buffer, count):
        total = buffer[0].astype(jnp.float32)
        for slot in range(1, count):
            total = total + buffer[slot].astype(jnp.float32)
        return total

    barrier = pltpu.get_barrier_semaphore()
    for target, count in ((at_z, nz), (at_y, ny), (at_era, ne)):
        for offset in range(1, count):
            pl.semaphore_signal(barrier, inc=1, device_id=target(offset), device_id_type=MESH)
    inputs = (
        (logp_in, logp),
        (topics_in, topics),
        (counts_in, counts),
        (bterm_in, bterm),
        (dyear_in, dyear),
        (drift_in, drift),
        (onoise_in, onoise),
    )
    loads = [pltpu.make_async_copy(src, dst, in_sems.at[index]) for index, (src, dst) in enumerate(inputs)]
    for load in loads:
        load.start()

    loads[1].wait()
    proportion = topics[...].astype(jnp.float32)
    proportion = proportion / jnp.sum(proportion, axis=1, keepdims=True)
    low[0][...] = proportion.astype(jnp.bfloat16)

    norm_z = spread_out(nzb, z, nz, at_z, nz_sems)
    norm_y = spread_out(nyb, y, ny, at_y, ny_sems)
    meta = spread_out(mbuf, z, nz, at_z, m_sems)

    hops = nz // 2
    items = 1 + max(len(part) for part in pieces)

    def ring_items(way, hop):
        need = blocks_needed(way, hop, ny, nz, nblk)
        return [0] + [1 + index for index, (_, end) in enumerate(pieces[way]) if end <= need]

    def ring_copy(way, hop, item):
        here = hop if way else (nz - hop) % nz
        there = hop + 1 if way else nz - hop - 1
        if item == 0:
            src, dst = low[here], low[there]
            if hop == hops - 1:
                half = pl.ds(way * (BLOCK // 2), BLOCK // 2)
                src, dst = src.at[half], dst.at[half]
        else:
            start, end = pieces[way][item - 1]
            block = pl.ds(nblk - end if way else start, end - start)
            src, dst = cnt[here].at[block], cnt[there].at[block]
        return remote(
            src, dst, ring_send.at[way, hop, item], ring_recv.at[way, hop, item], at_z(nz - 1 if way else 1)
        )

    def ring_pass(hop, which):
        for item in which:
            for way in range(2):
                if item in ring_items(way, hop):
                    ring_copy(way, hop, item).wait_recv()
                    if hop + 1 < hops and item in ring_items(way, hop + 1):
                        ring_copy(way, hop + 1, item).start()

    pl.semaphore_wait(barrier, nz + ny + ne - 3)
    for way in range(2):
        ring_copy(way, 0, 0).start()
    loads[0].wait()
    exponent = jnp.exp(logp[...].reshape(rows, BLOCK))
    expo[...] = exponent
    nzb[z] = row_sums(exponent)
    norm_z.start()

    for load in loads[2:]:
        load.wait()
    keys, antipodal = [], 0
    for index in range(nblk):
        distance = lax.rem(lax.rem(bterm[index], nz) - z + nz, nz)
        opposite = distance == hops
        key = jnp.where(distance < hops, -distance, nz - distance)
        keys.append(jnp.where(opposite, jnp.where(antipodal < ny // 2, -hops, hops), key))
        antipodal = antipodal + jnp.where(opposite, 1, 0)
    position = [0] * nblk
    for later in range(nblk):
        for earlier in range(later):
            before = jnp.where(keys[earlier] <= keys[later], 1, 0)
            position[later] = position[later] + before
            position[earlier] = position[earlier] + (1 - before)
    length = jnp.zeros((BLOCK, BLOCK), jnp.int32)
    filled = set()
    for step in range(max(len(part) for part in pieces)):
        for way in range(2):
            if step < len(pieces[way]):
                start, end = pieces[way][step]
                if way:
                    start, end = nblk - end, nblk - start
                for place in range(start, end):
                    if place not in filled:
                        filled.add(place)
                        block = sum(jnp.where(position[index] == place, index, 0) for index in range(nblk))
                        value = counts[block]
                        length = length + value
                        cnt[0][place] = value.astype(jnp.float32).astype(jnp.bfloat16)
                if 1 + step in ring_items(way, 0):
                    ring_copy(way, 0, 1 + step).start()
    lane = lax.broadcasted_iota(jnp.int32, (8, BLOCK), 1)
    table = jnp.full((8, BLOCK), nblk, jnp.int32)
    for index in range(nblk):
        table = jnp.where(lane == bterm[index], position[index], table)
    table = jnp.where(lane == ny * nz, lax.rem(dyear[0], years), table)
    mbuf[z] = table
    meta.start()
    for slot in range(nz):
        cnt[slot][nblk] = jnp.zeros((BLOCK, BLOCK), jnp.bfloat16)
    doc_length = jnp.sum(length.astype(jnp.float32), axis=1, keepdims=True)
    scale[...] = float(k) * proportion / doc_length
    cmat[...] = jnp.zeros_like(cmat)
    cmat[all_years : all_years + 1, :] = drift[...]
    cmat[all_years + 1 : all_years + 2, :] = onoise[...]

    norm_z.wait_recv()
    nyb[y] = total_of(nzb, nz)
    norm_y.start()
    norm_y.wait_recv()
    normalizer = jnp.transpose(jnp.broadcast_to(total_of(nyb, ny), (BLOCK, rows)))
    own_columns = pl.ds(pl.multiple_of(y * BLOCK, BLOCK), BLOCK)
    wbuf[:, :, own_columns] = (expo[...] / normalizer).astype(jnp.bfloat16).reshape(years, k, BLOCK)
    own_words = wbuf.at[:, :, own_columns]
    words = Copies(
        [
            remote(own_words, own_words, w_sems[0].at[offset - 1], w_sems[1].at[offset - 1], at_y(offset))
            for offset in range(1, ny)
        ]
    )
    words.start()

    totals = [jnp.zeros((1, k), jnp.float32) for _ in range(years)]
    sub_rows = rows // SUBS
    sub_topics = k // SUBS

    def stat_rows(sub, period):
        start = sub * sub_rows + period * sub_topics
        return slice(start, start + sub_topics)

    def document_block(slot):
        source = lax.rem(z + slot, nz)
        year = msmem[source, 0, ny * nz]
        left = low[slot][...]
        table = wbuf[year]
        scores = dot(left, table, ((1,), (0,)))
        here = slice(slot * BLOCK, (slot + 1) * BLOCK)
        for column in range(ny):
            block = cnt[slot][msmem[source, 0, column * nz + z]].astype(jnp.float32)
            terms = slice(column * BLOCK, (column + 1) * BLOCK)
            rall[here, terms] = (block / scores[:, terms]).astype(jnp.bfloat16)
        pull = dot(rall[here, :], table, ((1,), (1,)))
        left = left.astype(jnp.float32)
        share = jnp.sum(left * pull, axis=0, keepdims=True)
        turned = jnp.transpose(left)
        for period in range(years):
            flag = (year == period).astype(jnp.float32)
            masked = (turned * flag).astype(jnp.bfloat16)
            for sub in range(SUBS):
                ptall[stat_rows(sub, period), here] = masked[sub * sub_topics : (sub + 1) * sub_topics]
            totals[period] = totals[period] + share * flag
        if slot == 0:
            pbr[z] = pull.astype(jnp.bfloat16)
        else:
            pbs[slot] = pull.astype(jnp.bfloat16)

    order = [0]
    for step in range(1, hops):
        order += [step, nz - step]
    order.append(hops)
    last_doc = slice(hops * BLOCK, (hops + 1) * BLOCK)

    def first_product():
        columns = pl.ds(pl.multiple_of(lax.rem(y + ny // 2, ny) * BLOCK, BLOCK), BLOCK)
        before, after = slice(0, hops * BLOCK), slice((hops + 1) * BLOCK, nz * BLOCK)
        part = dot(ptall[:, before], rall[before, columns], ((1,), (0,)))
        if nz - 1 > hops:
            part = part + dot(ptall[:, after], rall[after, columns], ((1,), (0,)))
        expo[...] = part

    early = hops > 1
    done = 0
    for hop in range(hops):
        if hop == hops - 1 and early:
            first_product()
        last = hop == hops - 2 or hops == 1
        if last:
            ring_pass(hop, range(items // 2))
            words.wait_recv()
            meta.wait_recv()
            to_smem = pltpu.make_async_copy(mbuf, msmem, local_sem)
            to_smem.start()
            to_smem.wait()
            while done < min(3, 2 * hop + 1):
                document_block(order[done])
                done += 1
            ring_pass(hop, range(items // 2, items))
        else:
            ring_pass(hop, range(0 if hop == 0 else 0, items))
        if hop >= hops - 2:
            ready = nz if hop == hops - 1 else 2 * hop + 3
            while done < ready:
                document_block(order[done])
                done += 1

    tyb[y] = jnp.concatenate(totals, axis=1)
    total_y = spread_out(tyb, y, ny, at_y, ty_sems)
    total_z = spread_out(tzb, z, nz, at_z, tz_sems)
    total_era = spread_out(teb, era, ne, at_era, te_sems)
    total_y.start()

    stat_hops = ny // 2
    jump = stat_hops > 2

    def stat_subs(way, hop):
        if hop > 0:
            return list(range(SUBS))
        return list(range(SUBS // 2)) if way == 0 else list(range(SUBS // 2, SUBS))

    def stat_copy(way, hop, sub):
        part = pl.ds(sub * sub_rows, sub_rows)
        steps = 2 if jump and hop == 0 else 1
        return remote(
            sts.at[way, hop, part],
            str_.at[way, hop, part],
            st_sems[0].at[way, hop, sub],
            st_sems[1].at[way, hop, sub],
            at_y(ny - steps if way else steps),
        )

    def came_from(hop):
        if jump:
            return [[], [], [0, 1]][hop] if hop < 3 else [hop - 1]
        return [hop - 1] if hop else []

    def stat_block(offset):
        columns = pl.ds(pl.multiple_of(lax.rem(y + offset, ny) * BLOCK, BLOCK), BLOCK)
        if early and offset == stat_hops:
            part = expo[...] + dot(ptall[:, last_doc], rall[last_doc, columns], ((1,), (0,)))
        else:
            part = dot(ptall[...], rall[:, columns], ((1,), (0,)))
        words_here = [
            wbuf[period, sub * sub_topics : (sub + 1) * sub_topics, columns]
            for sub in range(SUBS)
            for period in range(years)
        ]
        return part * jnp.concatenate(words_here, axis=0).astype(jnp.float32)

    terms = float(ny * nz * BLOCK)
    pulls = Copies(
        [
            remote(pbs.at[offset], pbr.at[z], pb_sems[0].at[offset - 1], pb_sems[1].at[offset - 1], at_z(offset))
            for offset in range(1, nz)
        ]
    )

    def after_y():
        total_y.wait_recv()
        tzb[z] = total_of(tyb, ny)
        total_z.start()
        pulls.start()

    def after_z():
        total_z.wait_recv()
        teb[era] = jnp.log(terms) - jnp.log(total_of(tzb, nz) + terms)
        total_era.start()

    def after_era():
        total_era.wait_recv()
        for index in range(ne):
            for period in range(years):
                line = index * years + period
                cmat[line : line + 1, :] = teb[index, :, period * k : (period + 1) * k]
        cturn[...] = jnp.transpose(cmat[...])

    beside = [after_y, after_z, after_era]
    for hop in range(stat_hops):
        distance = stat_hops - hop
        parts = [stat_block(distance)]
        parts.append(parts[0] if hop == 0 else stat_block(ny - distance))
        for sub in range(SUBS):
            part = slice(sub * sub_rows, (sub + 1) * sub_rows)
            for way in range(2):
                if sub in stat_subs(way, hop):
                    value = parts[way][part]
                    for source in came_from(hop):
                        if sub in stat_subs(way, source):
                            stat_copy(way, source, sub).wait_recv()
                            value = value + str_[way, source, part, :].astype(jnp.float32)
                    sts[way, hop, part, :] = value.astype(jnp.bfloat16)
                    stat_copy(way, hop, sub).start()
        if hop > int(jump) and len(beside) > 1:
            beside.pop(0)()
    own_part = stat_block(0)
    while len(beside) > 1:
        beside.pop(0)()

    def slice_of(offset):
        return pl.ds(pl.multiple_of(lax.rem(era + offset, ne) * slice_rows, slice_rows), slice_rows)

    own_slice = slice_of(0)

    def level_copy(peer):
        return remote(es.at[peer], er.at[era], es_sems[0].at[peer], es_sems[1].at[era], {"era": peer})

    sent = 0
    for sub in range(SUBS):
        part = slice(sub * sub_rows, (sub + 1) * sub_rows)
        value = own_part[part]
        for way in range(2):
            if sub in stat_subs(way, stat_hops - 1):
                stat_copy(way, stat_hops - 1, sub).wait_recv()
                value = value + str_[way, stat_hops - 1, part, :].astype(jnp.float32)
        value = value.astype(jnp.bfloat16)
        step = min(slice_rows, sub_topics)
        for period in range(years):
            for start in range(0, sub_topics, step):
                topic = sub * sub_topics + start
                rows_here = slice(topic % slice_rows, topic % slice_rows + step)
                es[topic // slice_rows, period, rows_here, :] = value[
                    period * sub_topics + start : period * sub_topics + start + step
                ]
        while (sent + 1) * slice_rows <= (sub + 1) * sub_topics:
            pl.when(era != sent)(level_copy(sent).start)
            sent += 1
    er[era] = es[era]
    beside.pop(0)()
    columns = cturn[own_slice, :]

    def column(index):
        return jnp.broadcast_to(columns[:, index : index + 1], (slice_rows, BLOCK))

    spread = column(all_years)
    noise_scale = column(all_years + 1)
    for early_copies in (norm_z, meta, norm_y, words, total_y):
        early_copies.wait_send()
    for hop in range(hops):
        for item in range(items):
            for way in range(2):
                if item in ring_items(way, hop):
                    ring_copy(way, hop, item).wait_send()
    for offset in range(1, ne):
        sender = lax.rem(era + offset, ne)
        remote(es.at[sender], er.at[sender], es_sems[0].at[sender], es_sems[1].at[sender], at_era(offset)).wait_recv()

    variance = jnp.full((slice_rows, BLOCK), PRIOR_VARIANCE, jnp.float32)
    mean = jnp.zeros((slice_rows, BLOCK), jnp.float32)
    means, weights = [], []
    for period in range(all_years):
        level = jnp.log(er[period // years, period % years].astype(jnp.float32) + 1.0)
        observed = level + column(period)
        noise = noise_scale / (1.0 + level)
        predicted = variance + spread
        gain = predicted / (predicted + noise)
        mean = mean + gain * (observed - mean)
        variance = gain * noise
        means.append(mean)
        weights.append(variance / (variance + spread))
    smooth = means[-1]
    sm[ne - 1, years - 1] = smooth.astype(sm.dtype)
    for period in range(all_years - 2, -1, -1):
        smooth = means[period] + weights[period] * (smooth - means[period])
        sm[period // years, period % years] = smooth.astype(sm.dtype)

    land[era] = sm[era]
    results = Copies(
        [
            remote(
                sm.at[lax.rem(era + offset, ne)],
                land.at[era],
                out_sems[0].at[offset - 1],
                out_sems[1].at[offset - 1],
                at_era(offset),
            )
            for offset in range(1, ne)
        ]
    )
    results.start()
    pulls.wait_recv()
    new_ref[...] = (scale[...] * total_of(pbr, nz)).astype(jnp.bfloat16)
    for sent in (total_z, total_era, pulls):
        sent.wait_send()
    for hop in range(stat_hops):
        for sub in range(SUBS):
            for way in range(2):
                if sub in stat_subs(way, hop):
                    stat_copy(way, hop, sub).wait_send()
    for offset in range(1, ne):
        level_copy(lax.rem(era + offset, ne)).wait_send()
    results.wait_recv()
    for index in range(ne):
        out_ref[:, index * slice_rows : (index + 1) * slice_rows, :] = land[index].astype(out_ref.dtype)
    results.wait_send()


def body(counts, block_term, doc_year, doc_topics, log_params, drift, obs_noise):
    ne = lax.axis_size("era")
    nz = NZ
    ny = lax.axis_size("dp") // nz
    years, k, _ = log_params.shape
    rows = years * k
    nblk = counts.shape[0]
    pieces = [ring_pieces(way, ny, nz, nblk) for way in range(2)]
    sizes = (ne, ny, nz, years, k, nblk, pieces)
    bf16, f32, i32 = jnp.bfloat16, jnp.float32, jnp.int32
    hops = nz // 2
    hbm = pl.BlockSpec(memory_space=pltpu.HBM)
    operands = (
        block_term,
        doc_year,
        counts,
        doc_topics,
        log_params,
        drift.reshape(1, -1),
        obs_noise.reshape(1, -1),
    )
    landing = [
        (pltpu.SMEM if index < 2 else pltpu.VMEM)(value.shape, value.dtype) for index, value in enumerate(operands)
    ]
    slots = [pltpu.VMEM((BLOCK, k), bf16)] * nz + [pltpu.VMEM((nblk + 1, BLOCK, BLOCK), bf16)] * nz
    work = [
        pltpu.VMEM((nz, 8, BLOCK), i32),
        pltpu.SMEM((nz, 8, BLOCK), i32),
        pltpu.VMEM((rows, BLOCK), f32),
        pltpu.VMEM((years, k, ny * BLOCK), bf16),
        pltpu.VMEM((nz, 1, rows), f32),
        pltpu.VMEM((ny, 1, rows), f32),
        pltpu.VMEM((BLOCK, k), f32),
        pltpu.VMEM((rows, nz * BLOCK), bf16),
        pltpu.VMEM((nz * BLOCK, ny * BLOCK), bf16),
        pltpu.VMEM((nz, BLOCK, k), bf16),
        pltpu.VMEM((nz, BLOCK, k), bf16),
        pltpu.VMEM((2, ny // 2, rows, BLOCK), bf16),
        pltpu.VMEM((2, ny // 2, rows, BLOCK), bf16),
        pltpu.VMEM((ny, 1, rows), f32),
        pltpu.VMEM((nz, 1, rows), f32),
        pltpu.VMEM((ne, 1, rows), f32),
        pltpu.VMEM((BLOCK, k), f32),
        pltpu.VMEM((k, BLOCK), f32),
        pltpu.VMEM((ne, years, k // ne, BLOCK), bf16),
        pltpu.VMEM((ne, years, k // ne, BLOCK), bf16),
        pltpu.VMEM((ne, years, k // ne, BLOCK), bf16),
        pltpu.VMEM((ne, years, k // ne, BLOCK), bf16),
    ]
    dma = pltpu.SemaphoreType.DMA
    ring_sems = dma((2, hops, 1 + max(len(part) for part in pieces)))
    sems = [dma((len(operands),)), ring_sems, ring_sems, dma]
    for count in (nz, ny, nz, ny, nz, 0, ny, nz, ne, ne + 1, ne):
        sems += [dma((count - 1,)) if count else dma((2, ny // 2, SUBS))] * 2
    new_topics, smoothed = pl.pallas_call(
        functools.partial(kernel, sizes),
        out_shape=(
            jax.ShapeDtypeStruct(doc_topics.shape, bf16),
            jax.ShapeDtypeStruct(log_params.shape, bf16),
        ),
        in_specs=[hbm] * len(operands),
        out_specs=(pl.BlockSpec(memory_space=pltpu.VMEM), pl.BlockSpec(memory_space=pltpu.VMEM)),
        scratch_shapes=landing + slots + work + sems,
        compiler_params=pltpu.CompilerParams(
            collective_id=0, has_side_effects=True, vmem_limit_bytes=60 * 1024 * 1024
        ),
    )(*operands)
    return (new_topics, smoothed.astype(f32))


def solution(mesh):
    return jax.shard_map(
        body,
        mesh=mesh,
        in_specs=(
            P(("era", "dp"), None, None),
            P(("era", "dp")),
            P(("era", "dp")),
            P(("era", "dp"), None),
            P("era", None, "dp"),
            P(),
            P(),
        ),
        out_specs=(P(("era", "dp"), None), P("era", None, "dp")),
        check_vma=False,
    )
```
